32 devices in a mesh: blk: 8 (over z, x), head: 4 (over y, core).
Axes of the slice: x: 2, y: 2, z: 4, core: 2. Of those that a mesh axis runs over, the one named last changes fastest.
Arguments:
- block_input: bfloat16 [2, 2048, 2048], P(None, ('blk', 'head')), may hold values from -6 to 6
- cotangent: bfloat16 [2, 2048, 2048], P(None, ('blk', 'head')), may hold values from -6 to 6
- w_query: bfloat16 [2048, 2048], P('blk', 'head'), may hold values from -0.125 to 0.125
- w_key: bfloat16 [2048, 2048], P('blk', 'head'), may hold values from -0.125 to 0.125
- w_value: bfloat16 [2048, 2048], P('blk', 'head'), may hold values from -0.125 to 0.125
- w_out: bfloat16 [2048, 2048], P('head', 'blk'), may hold values from -3 to 3
- w_gate: bfloat16 [2048, 8192], P('blk', 'head'), may hold values from -0.125 to 0.125
- w_up: bfloat16 [2048, 8192], P('blk', 'head'), may hold values from -0.125 to 0.125
- w_down: bfloat16 [8192, 2048], P('head', 'blk'), may hold values from -0.0625 to 0.0625
Outputs:
- block_output: bfloat16 [2, 2048, 2048], P(None, ('blk', 'head'))
- input_grad: bfloat16 [2, 2048, 2048], P(None, ('blk', 'head'))
- grad_query: float32 [2048, 2048], P('blk', 'head')
- grad_key: float32 [2048, 2048], P('blk', 'head')
- grad_value: float32 [2048, 2048], P('blk', 'head')
- grad_out: float32 [2048, 2048], P('head', 'blk')
- grad_gate: float32 [2048, 8192], P('blk', 'head')
- grad_up: float32 [2048, 8192], P('blk', 'head')
- grad_down: float32 [8192, 2048], P('head', 'blk')
The draws below stay inside these ranges and needn't reach their ends.
All inputs are finite; a program needn't handle non-finite values.
Results may differ from the reference program's by a relative error of at most 0.025.
Values may be sent and summed in bfloat16 or wider, within the bound.
No kernel may reach another device: no remote copies, remote signals or barrier semaphores. Data moves between devices by JAX's collectives and lax.ppermute only.
A program may use at most 256 MiB of HBM per device.

```python
import math
import jax
import jax.numpy as jnp
from jax import lax

D = 2048
HEADS = 16
HEAD_DIM = 128
FF = 8192
MICRO = 2
SEQ = 2048


def steps_of(stream_key, dims, cuts, least, top_value):
    factor_of = 1.0
    for axis_at, parts in cuts:
        steps = jax.random.uniform(jax.random.fold_in(jax.random.fold_in(stream_key, 6), axis_at), (parts,), jnp.float32, least / len(cuts), top_value / len(cuts))
        factor_of = factor_of * jnp.repeat(jnp.exp(steps), dims[axis_at] // parts).reshape((-1,) + (1,) * (len(dims) - 1 - axis_at))
    return factor_of


def bell_draw(rng, shape, width, reach, pieces=(), kind=jnp.bfloat16):
    values = width * jax.random.normal(rng, shape, jnp.float32)
    if pieces:
        values = values * steps_of(rng, shape, pieces, -0.22, 0.18)
    return jnp.clip(values, -reach, reach).astype(kind)


def setup_inputs(seed: int = 0) -> dict:
    key_list = jax.random.split(jax.random.key(seed), 10)
    return {
        "block_input": bell_draw(key_list[0], (MICRO, SEQ, D), 1.0, 6.0, ((1, 32),)),
        "cotangent": bell_draw(key_list[1], (MICRO, SEQ, D), 1.0, 6.0, ((1, 32),)),
        "w_query": bell_draw(key_list[2], (D, D), D ** -0.5, 0.125, ((0, 8), (1, 4))),
        "w_key": bell_draw(key_list[3], (D, D), D ** -0.5, 0.125, ((0, 8), (1, 4))),
        "w_value": bell_draw(key_list[4], (D, D), D ** -0.5, 0.125, ((0, 8), (1, 4))),
        "w_out": bell_draw(key_list[5], (D, D), (max(1, 4 * D // SEQ)) ** -0.5, 3.0, ((0, 4), (1, 8))),
        "w_gate": bell_draw(key_list[6], (D, FF), D ** -0.5, 0.125, ((0, 8), (1, 4))),
        "w_up": bell_draw(key_list[7], (D, FF), D ** -0.5, 0.125, ((0, 8), (1, 4))),
        "w_down": bell_draw(key_list[8], (FF, D), FF ** -0.5, 0.0625, ((0, 4), (1, 8))),
    }


epsilon = 1e-05
highest = lax.Precision.HIGHEST

@jax.custom_vjp
def low(v):
    return lax.optimization_barrier(v.astype(jnp.bfloat16)).astype(jnp.float32)

@jax.custom_vjp
def low_back(v):
    return v

def low_keep(v):
    return (low(v), None)

def low_pass(kept, grad):
    return (grad,)

def back_keep(v):
    return (v, None)

def back_low(kept, grad):
    return (low(grad),)
low.defvjp(low_keep, low_pass)
low_back.defvjp(back_keep, back_low)

def layer_norm(values):
    center = values - lax.optimization_barrier(jnp.mean(values, axis=-1, keepdims=True))
    spread = lax.optimization_barrier(jnp.mean(center * center, axis=-1, keepdims=True))
    return center * lax.rsqrt(spread + epsilon)

def rotary(values, places):
    half = values.shape[-1] // 2
    rates = 10000.0 ** (-jnp.arange(half, dtype=jnp.float32) * 2.0 / values.shape[-1])
    angles = places[:, None] * rates[None, :]
    cosine = jnp.cos(angles)[:, None, :]
    sine = jnp.sin(angles)[:, None, :]
    first = values[..., :half]
    second = values[..., half:]
    return jnp.concatenate([first * cosine - second * sine, second * cosine + first * sine], axis=-1)

def attend(query, key, value):
    length = query.shape[0]
    block = math.gcd(512, length)
    scale = HEAD_DIM ** (-0.5)
    places = jnp.arange(length, dtype=jnp.int32)

    def one_block(start):
        rows_query = lax.dynamic_slice_in_dim(query, start, block, 0)
        scores = low_back(jnp.einsum('rhd,nhd->hrn', rows_query, key, precision=highest) * scale)
        allowed = (start + jnp.arange(block, dtype=jnp.int32))[:, None] >= places[None, :]
        scores = jnp.where(allowed[None], scores, -1e+30)
        top = lax.optimization_barrier(jnp.max(scores, axis=-1, keepdims=True))
        weights = jnp.exp(scores - top)
        probs = weights / lax.optimization_barrier(jnp.sum(weights, axis=-1, keepdims=True))
        return jnp.einsum('hrn,nhd->rhd', low(probs), value, precision=highest)
    starts = jnp.arange(length // block, dtype=jnp.int32) * block
    blocks = lax.map(jax.checkpoint(one_block), starts)
    return blocks.reshape(length, HEADS * HEAD_DIM)

def layer(tokens, w_query, w_key, w_value, w_out, w_gate, w_up, w_down):
    length = tokens.shape[0]
    places = jnp.arange(length, dtype=jnp.int32).astype(jnp.float32)
    normed = low(layer_norm(tokens))
    query_raw = low_back(jnp.dot(normed, w_query, precision=highest))
    key_raw = low_back(jnp.dot(normed, w_key, precision=highest))
    query = low(rotary(query_raw.reshape(length, HEADS, HEAD_DIM), places))
    key = low(rotary(key_raw.reshape(length, HEADS, HEAD_DIM), places))
    value = low(low_back(jnp.dot(normed, w_value, precision=highest))).reshape(length, HEADS, HEAD_DIM)
    attended = low(low_back(attend(query, key, value)))
    mid = tokens + low_back(jnp.dot(attended, w_out, precision=highest))
    mid_normed = low(layer_norm(mid))
    gate = low_back(jnp.dot(mid_normed, w_gate, precision=highest))
    up = low_back(jnp.dot(mid_normed, w_up, precision=highest))
    hidden = low(jax.nn.silu(gate) * up)
    return mid + low_back(jnp.dot(hidden, w_down, precision=highest))

def reference(block_input, cotangent, w_query, w_key, w_value, w_out, w_gate, w_up, w_down):
    weights = tuple((item.astype(jnp.float32) for item in (w_query, w_key, w_value, w_out, w_gate, w_up, w_down)))

    def one_batch(sums, pair):
        tokens, back = pair
        output, pullback = jax.vjp(layer, tokens.astype(jnp.float32), weights[0], weights[1], weights[2], weights[3], weights[4], weights[5], weights[6])
        grads = pullback(back.astype(jnp.float32))
        sums = tuple((total + grad for total, grad in zip(sums, grads[1:])))
        return (sums, (output.astype(jnp.bfloat16), grads[0].astype(jnp.bfloat16)))
    initial = tuple((jnp.zeros(item.shape, jnp.float32) for item in weights))
    sums, stacked = lax.scan(one_batch, initial, (block_input, cotangent))
    return (stacked[0], stacked[1], sums[0], sums[1], sums[2], sums[3], sums[4], sums[5], sums[6])
```

```python
import functools

import jax
import jax.numpy as jnp
import numpy as np
from jax import lax
from jax.experimental import pallas as pl
from jax.experimental.pallas import tpu as pltpu
from jax.sharding import PartitionSpec as P

HEADS = 16
HEAD_DIM = 128
FF = 8192
AXES = ("blk", "head")
SCALE = HEAD_DIM**-0.5
EPS = 1e-05
F32 = jnp.float32
BF16 = jnp.bfloat16


def swap(value, nb, nh, db, dh):
    pairs = [
        (b * nh + h, (b ^ db) * nh + (h ^ dh)) for b in range(nb) for h in range(nh)
    ]
    return lax.ppermute(value, AXES, pairs)


def norm_stats(values):
    center = values - jnp.mean(values, axis=-1, keepdims=True)
    spread = jnp.mean(center * center, axis=-1, keepdims=True)
    rstd = lax.rsqrt(spread + EPS)
    return center * rstd, rstd


def norm_back(grad, normed, rstd):
    return (
        grad
        - jnp.mean(grad, axis=-1, keepdims=True)
        - normed * jnp.mean(grad * normed, axis=-1, keepdims=True)
    ) * rstd


def attend_kernel(q_ref, k_ref, v_ref, pq_ref, pk_ref, o_ref, lse_ref):
    scores = lax.dot_general(
        q_ref[...], k_ref[...], (((1,), (1,)), ((), ())), preferred_element_type=F32
    )
    scores = jnp.where(pk_ref[...] <= pq_ref[...], scores * SCALE, -1e30)
    top = jnp.max(scores, axis=-1, keepdims=True)
    weights = jnp.exp(scores - top)
    total = jnp.sum(weights, axis=-1, keepdims=True)
    summed = jnp.dot(weights.astype(BF16), v_ref[...], preferred_element_type=F32)
    o_ref[...] = (summed / total).astype(BF16)
    lse_ref[...] = top + jnp.log(total)


def attend_back_kernel(
    q_ref, do_ref, lse_ref, pq_ref, k_ref, v_ref, pk_ref, dq_ref, dk_ref, dv_ref
):
    @pl.when(pl.program_id(0) == 0)
    def _():
        dk_ref[...] = jnp.zeros_like(dk_ref)
        dv_ref[...] = jnp.zeros_like(dv_ref)

    q, k, v, do = q_ref[...], k_ref[...], v_ref[...], do_ref[...]
    scores = lax.dot_general(q, k, (((1,), (1,)), ((), ())), preferred_element_type=F32)
    probs = jnp.where(
        pk_ref[...] <= pq_ref[...], jnp.exp(scores * SCALE - lse_ref[...]), 0.0
    )
    dots = lax.dot_general(do, v, (((1,), (1,)), ((), ())), preferred_element_type=F32)
    delta = jnp.sum(probs * dots, axis=-1, keepdims=True)
    back = (probs * (dots - delta)).astype(BF16)
    dq_ref[...] = jnp.dot(back, k, preferred_element_type=F32) * SCALE
    dk_ref[...] += (
        lax.dot_general(back, q, (((0,), (0,)), ((), ())), preferred_element_type=F32)
        * SCALE
    )
    dv_ref[...] += lax.dot_general(
        probs.astype(BF16), do, (((0,), (0,)), ((), ())), preferred_element_type=F32
    )


def attend(q, k, v, pos_q, pos_k):
    rows, keys = q.shape[0], k.shape[0]
    bq = min(rows, max(64, (256 * 2048) // keys))
    row = lambda w: pl.BlockSpec((bq, w), lambda i: (i, 0))
    whole = lambda shape: pl.BlockSpec(shape, lambda i: (0, 0))
    return pl.pallas_call(
        attend_kernel,
        grid=(rows // bq,),
        in_specs=[
            row(HEAD_DIM),
            whole((keys, HEAD_DIM)),
            whole((keys, HEAD_DIM)),
            row(1),
            whole((1, keys)),
        ],
        out_specs=[row(HEAD_DIM), row(1)],
        out_shape=[
            jax.ShapeDtypeStruct((rows, HEAD_DIM), BF16),
            jax.ShapeDtypeStruct((rows, 1), F32),
        ],
        compiler_params=pltpu.CompilerParams(vmem_limit_bytes=48 * 2**20),
        cost_estimate=pl.CostEstimate(
            flops=4 * rows * keys * HEAD_DIM,
            bytes_accessed=8 * rows * HEAD_DIM,
            transcendentals=rows * keys,
        ),
        name="attend",
    )(q, k, v, pos_q, pos_k)


def attend_back(q, do, lse, pos_q, k, v, pos_k):
    rows, keys = q.shape[0], k.shape[0]
    bq = min(rows, max(64, (256 * 2048) // keys))
    row = lambda w: pl.BlockSpec((bq, w), lambda i: (i, 0))
    whole = lambda shape: pl.BlockSpec(shape, lambda i: (0, 0))
    kv = whole((keys, HEAD_DIM))
    return pl.pallas_call(
        attend_back_kernel,
        grid=(rows // bq,),
        in_specs=[row(HEAD_DIM), row(HEAD_DIM), row(1), row(1), kv, kv, whole((1, keys))],
        out_specs=[row(HEAD_DIM), kv, kv],
        out_shape=[
            jax.ShapeDtypeStruct((rows, HEAD_DIM), F32),
            jax.ShapeDtypeStruct((keys, HEAD_DIM), F32),
            jax.ShapeDtypeStruct((keys, HEAD_DIM), F32),
        ],
        compiler_params=pltpu.CompilerParams(vmem_limit_bytes=48 * 2**20),
        cost_estimate=pl.CostEstimate(
            flops=10 * rows * keys * HEAD_DIM,
            bytes_accessed=16 * rows * HEAD_DIM,
            transcendentals=rows * keys,
        ),
        name="attend_back",
    )(q, do, lse, pos_q, k, v, pos_k)


def rope(values, cosine, sine):
    half = HEAD_DIM // 2
    first, second = values[:, :half], values[:, half:]
    return jnp.concatenate(
        [first * cosine - second * sine, second * cosine + first * sine], axis=1
    )


def local(nb, nh, block_input, cotangent, w_query, w_key, w_value, w_out, w_gate, w_up, w_down):
    tok_rows, width = block_input.shape[1:]
    slices = HEADS // nh
    half = nb // 2
    spread = half // slices
    kin = width // nb
    unit = FF // HEADS
    b, h = lax.axis_index("blk"), lax.axis_index("head")
    low = b % slices
    second = b >= half
    mine = 2 * tok_rows
    move = functools.partial(swap, nb=nb, nh=nh)

    exchanges = ((1, 0), (2, 0), (0, 2))
    orders = [
        (exchanges[0], exchanges[2], exchanges[1], (0, 1)),
        (exchanges[2], exchanges[1], exchanges[0], (0, 1)),
        (exchanges[1], exchanges[0], exchanges[2], (0, 1)),
    ]
    cut = (3 * mine // 8) // 16 * 16
    counts = (cut, cut, mine - 2 * cut)
    starts = (0, cut, 2 * cut)

    def gather(value):
        parts = [value[s : s + n] for s, n in zip(starts, counts)]
        for step in range(4):
            arrived = [move(p, db=o[step][0], dh=o[step][1]) for p, o in zip(parts, orders)]
            parts = [jnp.concatenate([p, r], axis=0) for p, r in zip(parts, arrived)]
        return jnp.concatenate(parts, axis=0)

    def scatter(value):
        parts = [value[16 * s : 16 * (s + n)] for s, n in zip(starts, counts)]
        for step in (3, 2, 1, 0):
            kept = [p[: p.shape[0] // 2] for p in parts]
            sent = [p[p.shape[0] // 2 :] for p in parts]
            arrived = [move(p, db=o[step][0], dh=o[step][1]) for p, o in zip(sent, orders)]
            parts = [
                (p.astype(F32) + r.astype(F32)).astype(BF16) if step else p.astype(F32) + r.astype(F32)
                for p, r in zip(kept, arrived)
            ]
        return jnp.concatenate(parts, axis=0)

    flip_b, flip_h, place = [], [], []
    for order, s, n in zip(orders, starts, counts):
        db, dh = np.zeros(1, np.int32), np.zeros(1, np.int32)
        for x, y in order:
            db, dh = np.concatenate([db, db ^ x]), np.concatenate([dh, dh ^ y])
        rows = np.tile(np.arange(s, s + n), 16)
        flip_b.append(np.repeat(db, n) ^ np.where(rows >= tok_rows, half, 0))
        flip_h.append(np.repeat(dh, n))
        place.append(rows % tok_rows)
    flip_b, flip_h, place = map(np.concatenate, (flip_b, flip_h, place))

    def positions(block):
        return ((block ^ flip_b) * nh + (h ^ flip_h)) * tok_rows + place

    pos = positions(b)
    rates = 10000.0 ** (-jnp.arange(HEAD_DIM // 2, dtype=F32) * 2.0 / HEAD_DIM)
    angles = pos.astype(F32)[:, None] * rates[None, :]
    cosine, sine = jnp.cos(angles), jnp.sin(angles)

    def to_micro(pair):
        keep = jnp.where(second, pair[1], pair[0])
        send = jnp.where(second, pair[0], pair[1])
        return jnp.concatenate([keep, move(send, db=half, dh=0)], axis=0)

    def from_micro(rows):
        arrived = move(rows[tok_rows:], db=half, dh=0)
        kept = rows[:tok_rows]
        return jnp.stack(
            [jnp.where(second, arrived, kept), jnp.where(second, kept, arrived)]
        )

    def spread_weights(source):
        pieces = [lax.dynamic_index_in_dim(source, low, 0, False)]
        for d in range(1, slices):
            pieces.append(
                move(lax.dynamic_index_in_dim(source, low ^ d, 0, False), db=d, dh=0)
            )
        step = slices
        while step < nb:
            arrived = move(jnp.stack(pieces), db=step, dh=0)
            pieces = pieces + [arrived[i] for i in range(len(pieces))]
            step *= 2
        return pieces

    def in_order(pieces, lo, hi):
        result = jnp.zeros((len(pieces), kin, hi - lo), BF16)
        for j, piece in enumerate(pieces):
            result = lax.dynamic_update_index_in_dim(result, piece[:, lo:hi], b ^ j, 0)
        return result

    def by_slice(weight):
        return weight.reshape(kin, slices, -1).transpose(1, 0, 2)

    def fold_rows(block, tall):
        n = block.shape[0]
        if tall >= kin:
            return block.reshape(n, tall // kin, kin, kin).transpose(0, 2, 1, 3).reshape(n, kin, tall)
        return block.reshape(n, tall, kin // tall, tall).transpose(0, 2, 1, 3).reshape(n, kin, tall)

    def unfold_rows(block, tall):
        n = block.shape[0]
        if tall >= kin:
            return block.reshape(n, kin, tall // kin, kin).transpose(2, 1, 0, 3).reshape(tall, n * kin)
        return block.reshape(n, kin // tall, tall, tall).transpose(2, 0, 1, 3).reshape(tall, n * kin)

    def refold_rows(grad, tall):
        if tall >= kin:
            return grad.reshape(tall // kin, kin, nb, kin).transpose(2, 1, 0, 3).reshape(nb, kin, tall)
        return grad.reshape(tall, nb, kin // tall, tall).transpose(1, 2, 0, 3).reshape(nb, kin, tall)

    def from_fold(block, tall):
        n = block.shape[0]
        if tall >= kin:
            return block.reshape(n, kin, tall // kin, kin).transpose(0, 2, 1, 3).reshape(n, tall, kin)
        return block.reshape(n, kin // tall, tall, tall).transpose(0, 2, 1, 3).reshape(n, tall, kin)

    tokens = to_micro(block_input).astype(F32)
    attn_source = jnp.concatenate(
        [
            by_slice(w_query),
            by_slice(w_key),
            by_slice(w_value),
            fold_rows(w_out.reshape(slices, HEAD_DIM, kin), HEAD_DIM),
        ],
        axis=2,
    )
    attn_pieces = spread_weights(attn_source)
    back_rows = to_micro(cotangent)
    feed_source = jnp.concatenate(
        [by_slice(w_gate), by_slice(w_up), fold_rows(w_down.reshape(slices, unit, kin), unit)],
        axis=2,
    )
    feed_pieces = spread_weights(feed_source)

    w_joined = in_order(attn_pieces, 0, 3 * HEAD_DIM).reshape(width, 3 * HEAD_DIM)
    w_out_rows = unfold_rows(in_order(attn_pieces, 3 * HEAD_DIM, 4 * HEAD_DIM), HEAD_DIM)
    w_paired = in_order(feed_pieces, 0, 2 * unit).reshape(width, 2 * unit)
    w_down_rows = unfold_rows(in_order(feed_pieces, 2 * unit, 3 * unit), unit)

    normed_f, rstd_in = norm_stats(tokens)
    normed_all = gather(normed_f.astype(BF16))
    projected = jnp.dot(normed_all, w_joined, preferred_element_type=F32)
    query = rope(projected[:, :HEAD_DIM], cosine, sine).astype(BF16)
    key = rope(projected[:, HEAD_DIM : 2 * HEAD_DIM], cosine, sine).astype(BF16)
    value = projected[:, 2 * HEAD_DIM :].astype(BF16)

    if spread > 1:
        teams = [
            [(((m * spread + s) * slices + l) * nh + k) for s in range(spread)]
            for m in range(2)
            for l in range(slices)
            for k in range(nh)
        ]
        everyone = lambda t: lax.all_gather(t, AXES, axis=0, tiled=True, axis_index_groups=teams)
        keys, values = everyone(key), everyone(value)
        first = b - (b // slices % spread) * slices
        pos_k = jnp.concatenate([positions(first + s * slices) for s in range(spread)])
    else:
        keys, values, pos_k = key, value, pos

    attended, lse = attend(query, keys, values, pos[:, None], pos_k[None, :])
    mixed = scatter(jnp.dot(attended, w_out_rows, preferred_element_type=F32).astype(BF16))
    mid = tokens + mixed
    mid_f, rstd_mid = norm_stats(mid)
    back_all = gather(back_rows)
    mid_all = gather(mid_f.astype(BF16))
    gate_up = jnp.dot(mid_all, w_paired, preferred_element_type=F32)
    gate, up = gate_up[:, :unit], gate_up[:, unit:]
    sig = 1.0 / (1.0 + jnp.exp(-gate))
    hidden = (gate * sig * up).astype(BF16)
    back_hidden = lax.dot_general(
        back_all, w_down_rows, (((1,), (1,)), ((), ())), preferred_element_type=F32
    )
    back_gate = back_hidden * up * sig * (1.0 + gate * (1.0 - sig))
    back_up = back_hidden * gate * sig
    back_paired = jnp.concatenate([back_gate, back_up], axis=1).astype(BF16)
    back_mid_normed = scatter(
        lax.dot_general(
            back_paired, w_paired, (((1,), (1,)), ((), ())), preferred_element_type=F32
        ).astype(BF16)
    )
    output = mid + scatter(
        jnp.dot(hidden, w_down_rows, preferred_element_type=F32).astype(BF16)
    )
    block_output = from_micro(output.astype(BF16))

    over_rows = (((0,), (0,)), ((), ()))
    grad_down = lax.dot_general(hidden, back_all, over_rows, preferred_element_type=F32)
    grad_feed = lax.dot_general(mid_all, back_paired, over_rows, preferred_element_type=F32)

    def collect(grads):
        step = half
        while step >= slices:
            grads = grads.reshape((2, grads.shape[0] // 2) + grads.shape[1:])
            bit = (b // step) % 2
            kept = lax.dynamic_index_in_dim(grads, bit, 0, False)
            sent = lax.dynamic_index_in_dim(grads, 1 - bit, 0, False)
            grads = (kept.astype(F32) + move(sent, db=step, dh=0).astype(F32)).astype(BF16)
            step //= 2
        result = lax.dynamic_update_index_in_dim(
            jnp.zeros_like(grads), lax.dynamic_index_in_dim(grads, low, 0, False), low, 0
        )
        for d in range(1, slices):
            arrived = move(lax.dynamic_index_in_dim(grads, low ^ d, 0, False), db=d, dh=0)
            result = lax.dynamic_update_index_in_dim(result, arrived, low ^ d, 0)
        return result

    def to_shard(block):
        return block.transpose(1, 0, 2).reshape(kin, -1).astype(F32)

    feed_sum = collect(
        jnp.concatenate(
            [
                grad_feed.astype(BF16).reshape(nb, kin, 2 * unit),
                refold_rows(grad_down.astype(BF16), unit),
            ],
            axis=2,
        )
    )
    grad_gate = to_shard(feed_sum[:, :, :unit])
    grad_up = to_shard(feed_sum[:, :, unit : 2 * unit])
    grad_down_shard = from_fold(feed_sum[:, :, 2 * unit :], unit).reshape(slices * unit, kin).astype(F32)

    back_mid = back_rows.astype(F32) + norm_back(back_mid_normed, mid_f, rstd_mid)
    back_attn_all = gather(back_mid.astype(BF16))
    grad_out = lax.dot_general(attended, back_attn_all, over_rows, preferred_element_type=F32)
    back_attended = lax.dot_general(
        back_attn_all, w_out_rows, (((1,), (1,)), ((), ())), preferred_element_type=F32
    ).astype(BF16)
    back_q, back_k, back_v = attend_back(
        query, back_attended, lse, pos[:, None], keys, values, pos_k[None, :]
    )
    if spread > 1:
        shared = lambda t: lax.psum_scatter(
            t, AXES, scatter_dimension=0, tiled=True, axis_index_groups=teams
        )
        back_k, back_v = shared(back_k), shared(back_v)
    back_joined = jnp.concatenate(
        [rope(back_q, cosine, -sine), rope(back_k, cosine, -sine), back_v], axis=1
    ).astype(BF16)
    back_normed = scatter(
        lax.dot_general(
            back_joined, w_joined, (((1,), (1,)), ((), ())), preferred_element_type=F32
        ).astype(BF16)
    )
    grad_joined = lax.dot_general(normed_all, back_joined, over_rows, preferred_element_type=F32)
    attn_sum = collect(
        jnp.concatenate(
            [
                grad_joined.astype(BF16).reshape(nb, kin, 3 * HEAD_DIM),
                refold_rows(grad_out.astype(BF16), HEAD_DIM),
            ],
            axis=2,
        )
    )
    input_grad = from_micro((back_mid + norm_back(back_normed, normed_f, rstd_in)).astype(BF16))
    return (
        block_output,
        input_grad,
        to_shard(attn_sum[:, :, :HEAD_DIM]),
        to_shard(attn_sum[:, :, HEAD_DIM : 2 * HEAD_DIM]),
        to_shard(attn_sum[:, :, 2 * HEAD_DIM : 3 * HEAD_DIM]),
        from_fold(attn_sum[:, :, 3 * HEAD_DIM :], HEAD_DIM)
        .reshape(slices * HEAD_DIM, kin)
        .astype(F32),
        grad_gate,
        grad_up,
        grad_down_shard,
    )


def solution(mesh):
    rows = P(None, AXES, None)
    placed = (rows, rows) + (P("blk", "head"),) * 3 + (P("head", "blk"),) + (P("blk", "head"),) * 2 + (P("head", "blk"),)
    return jax.shard_map(
        functools.partial(local, mesh.shape["blk"], mesh.shape["head"]),
        mesh=mesh,
        in_specs=placed,
        out_specs=placed,
        check_vma=False,
    )
```

```python
import functools

import jax
import jax.numpy as jnp
import numpy as np
from jax import lax
from jax.experimental import pallas as pl
from jax.experimental.pallas import tpu as pltpu
from jax.sharding import PartitionSpec as P

HEADS = 16
HEAD_DIM = 128
FF = 8192
AXES = ("blk", "head")
SCALE = HEAD_DIM**-0.5
EPS = 1e-05
F32 = jnp.float32
BF16 = jnp.bfloat16
VMEM = pl.BlockSpec(memory_space=pltpu.VMEM)
SMEM = pl.BlockSpec(memory_space=pltpu.SMEM)
NN = (((1,), (0,)), ((), ()))
NT = (((1,), (1,)), ((), ()))
TN = (((0,), (0,)), ((), ()))


def dot(a, b, dims=NN):
    return lax.dot_general(a, b, dims, preferred_element_type=F32)


def shape(rows, columns, kind=BF16):
    return jax.ShapeDtypeStruct((rows, columns), kind)


def call(kernel, outs, name, flops=0, moved=0, grid=None, **more):
    settings = dict(
        out_shape=outs,
        compiler_params=pltpu.CompilerParams(vmem_limit_bytes=56 * 2**20),
        name=name,
    )
    if flops:
        settings["cost_estimate"] = pl.CostEstimate(
            flops=int(flops), bytes_accessed=int(moved), transcendentals=0
        )
    settings.update(more)
    if grid is not None:
        settings["grid"] = grid
    return pl.pallas_call(kernel, **settings)


def swap(value, nb, nh, db, dh):
    pairs = [
        (b * nh + h, (b ^ db) * nh + (h ^ dh)) for b in range(nb) for h in range(nh)
    ]
    return lax.ppermute(value, AXES, pairs)


def norm_stats(values):
    center = values - jnp.mean(values, axis=-1, keepdims=True)
    spread = jnp.mean(center * center, axis=-1, keepdims=True)
    rstd = lax.rsqrt(spread + EPS)
    return center * rstd, rstd


def norm_back(grad, normed, rstd):
    return (
        grad
        - jnp.mean(grad, axis=-1, keepdims=True)
        - normed * jnp.mean(grad * normed, axis=-1, keepdims=True)
    ) * rstd


def turn(values, table, back=False):
    half = HEAD_DIM // 2
    other = jnp.concatenate([values[:, half:], values[:, :half]], axis=1)
    other = other * table[:, HEAD_DIM:]
    return values * table[:, :HEAD_DIM] + (-other if back else other)


def after(value, *others):
    return lax.optimization_barrier((value,) + others)[0]


def pack(low, weights, slices, kin):
    wide = [w.shape[1] // slices for w in weights[:-1]]
    wide.append(weights[-1].shape[0] // slices)
    total = sum(wide)

    def kernel(low_ref, *refs):
        sources, outs = refs[: len(weights)], refs[len(weights) :]
        for d in range(slices):
            at = 0
            which = low_ref[0] ^ d
            for i, (source, w) in enumerate(zip(sources, wide)):
                where = pl.ds(pl.multiple_of(which * w, 128), w)
                if i < len(wide) - 1:
                    outs[d][:, at : at + w] = source[:, where]
                else:
                    outs[d][:, at : at + w] = source[where, :].T
                at += w

    return call(
        kernel,
        [shape(kin, total)] * slices,
        "pack",
        in_specs=[SMEM] + [VMEM] * len(weights),
        out_specs=[VMEM] * slices,
    )(low, *weights)


def assemble(low, pieces, kin, slices):
    groups = pieces[0][0].shape[0] // (kin * len(pieces[0][1]))
    total = pieces[0][0].shape[1]

    def kernel(low_ref, *refs):
        out = refs[-1]
        for (_, which), piece in zip(pieces, refs):
            for g in range(groups):
                for i, d in enumerate(which):
                    block = g * slices + (low_ref[0] ^ d)
                    rows = pl.ds(pl.multiple_of(block * kin, kin), kin)
                    at = (g * len(which) + i) * kin
                    out[rows, :] = piece[at : at + kin, :]

    return call(
        kernel,
        shape(groups * slices * kin, total),
        "assemble",
        in_specs=[SMEM] + [VMEM] * len(pieces),
        out_specs=VMEM,
    )(low, *[p for p, _ in pieces])


def unpack(low, pieces, wide):
    kin, slices = pieces[0].shape[0], len(pieces)

    def kernel(low_ref, *refs):
        sources, outs = refs[:slices], refs[slices:]
        for d in range(slices):
            at = 0
            which = low_ref[0] ^ d
            for i, (out, w) in enumerate(zip(outs, wide)):
                where = pl.ds(pl.multiple_of(which * w, 128), w)
                part = sources[d][:, at : at + w].astype(F32)
                if i < len(wide) - 1:
                    out[:, where] = part
                else:
                    out[where, :] = part.T
                at += w

    outs = [shape(kin, slices * w, F32) for w in wide[:-1]]
    outs.append(shape(slices * wide[-1], kin, F32))
    return call(
        kernel,
        outs,
        "unpack",
        in_specs=[SMEM] + [VMEM] * slices,
        out_specs=[VMEM] * len(wide),
    )(low, *pieces)


def join(refs):
    return jnp.concatenate([r[...] for r in refs], axis=0)


def project(pieces, weights, table):
    section = pieces[0].shape[0] * 2
    sections = len(pieces) // 2
    rows = section * sections

    def kernel(*refs):
        parts, (w, t, q, k, v) = refs[: len(pieces)], refs[len(pieces) :]
        for s in range(sections):
            out = dot(join(parts[2 * s : 2 * s + 2]), w[:, : 3 * HEAD_DIM])
            at = pl.ds(s * section, section)
            angles = t[at, :]
            q[at, :] = turn(out[:, :HEAD_DIM], angles).astype(BF16)
            k[at, :] = turn(out[:, HEAD_DIM : 2 * HEAD_DIM], angles).astype(BF16)
            v[at, :] = out[:, 2 * HEAD_DIM :].astype(BF16)

    width = weights.shape[0]
    return call(
        kernel,
        [shape(rows, HEAD_DIM)] * 3,
        "project",
        6 * rows * width * HEAD_DIM,
        2 * rows * width,
        in_specs=[VMEM] * (len(pieces) + 2),
        out_specs=[VMEM] * 3,
    )(*pieces, weights, table)


def row_block(keys):
    return max(64, 256 * 2048 // keys)


def split_rows(rows, step, width):
    n = rows // 2 // step
    return (
        n,
        [
            pl.BlockSpec((step, width), lambda i: (jnp.minimum(i, n - 1), 0)),
            pl.BlockSpec((step, width), lambda i: (jnp.maximum(i - n, 0), 0)),
        ],
        [shape(rows // 2, width)] * 2,
    )


def put(n, kept, sent, value):
    @pl.when(pl.program_id(0) < n)
    def _():
        kept[...] = value

    @pl.when(pl.program_id(0) >= n)
    def _():
        sent[...] = value


def attend(q, k, v, weights, pos_q, pos_k, half):
    rows, keys, width = q.shape[0] // 2, k.shape[0], weights.shape[0]
    bq = min(rows // 2, row_block(keys))
    first = half * rows // bq
    n, split, shapes = split_rows(rows, bq, width)

    def kernel(q_ref, k_ref, v_ref, w_ref, pq_ref, pk_ref, o_ref, lse_ref, kept, sent):
        scores = dot(q_ref[...], k_ref[...], NT)
        scores = jnp.where(pk_ref[...] <= pq_ref[...], scores * SCALE, -1e30)
        top = jnp.max(scores, axis=-1, keepdims=True)
        probs = jnp.exp(scores - top)
        total = jnp.sum(probs, axis=-1, keepdims=True)
        low = (dot(probs.astype(BF16), v_ref[...]) / total).astype(BF16)
        o_ref[...] = low
        lse_ref[...] = top + jnp.log(total)
        put(n, kept, sent, dot(low, w_ref[:, 3 * HEAD_DIM :], NT).astype(BF16))

    there = lambda w: pl.BlockSpec((bq, w), lambda i: (i + first, 0))
    here = lambda w: pl.BlockSpec((bq, w), lambda i: (i, 0))
    whole = lambda a: pl.BlockSpec(a.shape, lambda i: (0, 0))
    return call(
        kernel,
        [shape(rows, HEAD_DIM), shape(rows, 1, F32)] + shapes,
        "attend",
        4 * rows * keys * HEAD_DIM + 2 * rows * width * HEAD_DIM,
        2 * rows * width,
        grid=(rows // bq,),
        in_specs=[there(HEAD_DIM), whole(k), whole(v), whole(weights), there(1), whole(pos_k)],
        out_specs=[here(HEAD_DIM), here(1)] + split,
    )(q, k, v, weights, pos_q, pos_k)


def feed(tokens, backs, weights):
    rows, width = sum(p.shape[0] for p in tokens), weights.shape[0]
    unit = weights.shape[1] // 3
    count = len(tokens)
    step = min(256, rows // 2)

    def kernel(*refs):
        xs, gs = refs[:count], refs[count : 2 * count]
        w, paired, hidden, kept, sent, x_all, g_all = refs[2 * count :]
        at = 0
        for x, g in zip(xs, gs):
            x_all[at : at + x.shape[0], :] = x[...]
            g_all[at : at + x.shape[0], :] = g[...]
            at += x.shape[0]

        for first, part in ((0, kept), (rows // 2, sent)):

            @pl.loop(0, rows // 2 // step)
            def _(i):
                at = pl.ds(pl.multiple_of(first + i * step, step), step)
                gate_up = dot(x_all[at, :], w[:, : 2 * unit])
                back = dot(g_all[at, :], w[:, 2 * unit :])
                gate, up = gate_up[:, :unit], gate_up[:, unit:]
                sig = 1.0 / (1.0 + jnp.exp(-gate))
                act = gate * sig
                hidden[at, :] = (act * up).astype(BF16)
                paired[at, :unit] = (back * up * sig * (1.0 + gate * (1.0 - sig))).astype(BF16)
                paired[at, unit:] = (back * act).astype(BF16)
                there = pl.ds(pl.multiple_of(i * step, step), step)
                part[there, :] = dot(paired[at, :], w[:, : 2 * unit], NT).astype(BF16)

    return call(
        kernel,
        [shape(rows, 2 * unit), shape(rows, unit)] + [shape(rows // 2, width)] * 2,
        "feed",
        10 * rows * unit * width,
        2 * rows * width,
        in_specs=[VMEM] * (2 * count + 1),
        out_specs=[VMEM] * 4,
        scratch_shapes=[pltpu.VMEM((rows, width), BF16)] * 2,
    )(*tokens, *backs, weights)


def feed_out(hidden, weights):
    rows, unit = hidden.shape
    width = weights.shape[0]
    step = min(256, rows // 2)
    n, split, shapes = split_rows(rows, step, width)

    def kernel(hidden_ref, w_ref, kept, sent):
        put(n, kept, sent, dot(hidden_ref[...], w_ref[:, 2 * unit :], NT).astype(BF16))

    return call(
        kernel,
        shapes,
        "feed_out",
        2 * rows * unit * width,
        2 * rows * width,
        grid=(rows // step,),
        in_specs=[
            pl.BlockSpec((step, unit), lambda i: (i, 0)),
            pl.BlockSpec(weights.shape, lambda i: (0, 0)),
        ],
        out_specs=split,
    )(hidden, weights)


def weight_grads(pairs, width):
    columns = [sides[0].shape[1] for _, sides in pairs]
    total = sum(columns)
    block = 256
    flat = []
    for pieces, sides in pairs:
        flat += list(pieces) + list(sides)

    def kernel(*refs):
        out = refs[-1]
        at, start = 0, 0
        for (pieces, sides), wide in zip(pairs, columns):
            left = join(refs[at : at + len(pieces)])
            at += len(pieces)
            right = join(refs[at : at + len(sides)])
            at += len(sides)
            out[:, start : start + wide] = dot(left, right, TN).astype(BF16)
            start += wide

    specs = []
    for pieces, sides in pairs:
        specs += [pl.BlockSpec((p.shape[0], block), lambda j: (0, j)) for p in pieces]
        specs += [pl.BlockSpec(s.shape, lambda j: (0, 0)) for s in sides]
    rows = sum(p.shape[0] for p in pairs[0][0])
    return call(
        kernel,
        shape(width, total),
        "weight_grads",
        2 * rows * width * total,
        2 * rows * (width + total),
        grid=(width // block,),
        in_specs=specs,
        out_specs=pl.BlockSpec((block, total), lambda j: (j, 0)),
    )(*flat)


def back_project(pieces, weights):
    rows, width = sum(p.shape[0] for p in pieces), weights.shape[0]

    def kernel(*refs):
        w, out = refs[-2:]
        at = 0
        for s in range(len(pieces) // 2):
            x = join(refs[2 * s : 2 * s + 2])
            out[at : at + x.shape[0], :] = dot(x, w[:, 3 * HEAD_DIM :]).astype(BF16)
            at += x.shape[0]

    return call(
        kernel,
        shape(rows, HEAD_DIM),
        "back_project",
        2 * rows * width * HEAD_DIM,
        2 * rows * width,
        in_specs=[VMEM] * (len(pieces) + 1),
        out_specs=VMEM,
    )(*pieces, weights)


def attend_back(q, do, lse, pos_q, k, v, pos_k):
    rows, keys = q.shape[0], k.shape[0]
    bq = min(rows, row_block(keys))

    def kernel(q_ref, do_ref, lse_ref, pq_ref, k_ref, v_ref, pk_ref, dq_ref, dk_ref, dv_ref):
        @pl.when(pl.program_id(0) == 0)
        def _():
            dk_ref[...] = jnp.zeros_like(dk_ref)
            dv_ref[...] = jnp.zeros_like(dv_ref)

        q, k, v, do = q_ref[...], k_ref[...], v_ref[...], do_ref[...]
        scores = dot(q, k, NT)
        probs = jnp.where(
            pk_ref[...] <= pq_ref[...], jnp.exp(scores * SCALE - lse_ref[...]), 0.0
        )
        dots = dot(do, v, NT)
        delta = jnp.sum(probs * dots, axis=-1, keepdims=True)
        back = (probs * (dots - delta)).astype(BF16)
        dq_ref[...] = dot(back, k) * SCALE
        dk_ref[...] += dot(back, q, TN) * SCALE
        dv_ref[...] += dot(probs.astype(BF16), do, TN)

    row = lambda w: pl.BlockSpec((bq, w), lambda i: (i, 0))
    whole = lambda s: pl.BlockSpec(s, lambda i: (0, 0))
    kv = whole((keys, HEAD_DIM))
    return call(
        kernel,
        [shape(rows, HEAD_DIM, F32), shape(keys, HEAD_DIM, F32), shape(keys, HEAD_DIM, F32)],
        "attend_back",
        10 * rows * keys * HEAD_DIM,
        16 * rows * HEAD_DIM,
        grid=(rows // bq,),
        in_specs=[row(HEAD_DIM), row(HEAD_DIM), row(1), row(1), kv, kv, whole((1, keys))],
        out_specs=[row(HEAD_DIM), kv, kv],
    )(q, do, lse, pos_q, k, v, pos_k)


def back_input(dq, dk, dv, table, weights, half):
    rows, width = dq.shape[0] // 2, weights.shape[0]
    step = min(256, rows // 2)
    first = half * rows // step
    n, split, shapes = split_rows(rows, step, width)

    def kernel(dq_ref, dk_ref, dv_ref, t_ref, w_ref, joined, kept, sent):
        joined[:, :HEAD_DIM] = turn(dq_ref[...], t_ref[...], True).astype(BF16)
        joined[:, HEAD_DIM : 2 * HEAD_DIM] = turn(dk_ref[...], t_ref[...], True).astype(BF16)
        joined[:, 2 * HEAD_DIM :] = dv_ref[...].astype(BF16)
        put(n, kept, sent, dot(joined[...], w_ref[:, : 3 * HEAD_DIM], NT).astype(BF16))

    there = lambda w: pl.BlockSpec((step, w), lambda i: (i + first, 0))
    here = lambda w: pl.BlockSpec((step, w), lambda i: (i, 0))
    return call(
        kernel,
        [shape(rows, 3 * HEAD_DIM)] + shapes,
        "back_input",
        6 * rows * width * HEAD_DIM,
        2 * rows * width,
        grid=(rows // step,),
        in_specs=[there(HEAD_DIM)] * 3
        + [there(2 * HEAD_DIM), pl.BlockSpec(weights.shape, lambda i: (0, 0))],
        out_specs=[here(3 * HEAD_DIM)] + split,
    )(dq, dk, dv, table, weights)


def local(nb, nh, block_input, cotangent, w_query, w_key, w_value, w_out, w_gate, w_up, w_down):
    tok_rows, width = block_input.shape[1:]
    slices = HEADS // nh
    half = nb // 2
    groups = nb // slices
    spread = groups // 2
    kin = width // nb
    unit = FF // HEADS
    b, h = lax.axis_index("blk"), lax.axis_index("head")
    low, group = b % slices, b // slices
    second = b >= half
    mine = 2 * tok_rows
    move = functools.partial(swap, nb=nb, nh=nh)
    scalar = lambda v: v.astype(jnp.int32).reshape(1)

    opening, core = (2, 0), (0, 1)
    orders = [((1, 0), (0, 2)), ((0, 2), (1, 0))]

    def exchange(values, step):
        return [move(v, db=o[step][0], dh=o[step][1]) for v, o in zip(values, orders)]

    def across(value, way):
        return move(value, db=way[0], dh=way[1])

    def tied(values, beside):
        return [after(v, *beside) for v in values] if beside else values

    class Gather:
        def __init__(self, value):
            self.parts = value
            self.sent = across(value, opening)

        def open(self, *beside):
            arrived = tied([self.sent], beside)[0]
            n = tok_rows
            self.parts = [
                jnp.concatenate([self.parts[:n], arrived[:n]], axis=0),
                jnp.concatenate([self.parts[n:], arrived[n:]], axis=0),
            ]
            self.sent = exchange(self.parts, 0)

        def take(self, *beside):
            arrived = tied(self.sent, beside)
            self.parts = [jnp.concatenate([p, r], axis=0) for p, r in zip(self.parts, arrived)]
            self.sent = exchange(self.parts, 1)
            self.near = self.parts + [across(p, core) for p in self.parts]

        def far(self, *beside):
            pieces = tied(self.sent, beside)
            return pieces + [across(p, core) for p in pieces]

    def gather(value):
        work = Gather(value)
        work.open()
        work.take()
        return work.near, work.far()

    class Scatter:
        def __init__(self, kept, sent):
            self.kept, self.sent = kept, across(sent, core)

        def add(self, *beside):
            arrived = tied([self.sent], beside)[0]
            n = self.kept.shape[0] // 2
            return [
                (self.kept[r].astype(F32) + arrived[r].astype(F32)).astype(BF16)
                for r in (slice(0, n), slice(n, 2 * n))
            ]

        def open(self, *beside):
            self.far = self.add(*beside)
            self.sent_far = exchange(self.far, 1)

        def near(self, kept, sent):
            self.kept, self.sent = kept, across(sent, core)

        def take_near(self, *beside):
            self.parts = self.add(*beside)

        def take(self, *beside):
            arrived = tied(self.sent_far, beside)
            sums = [p.astype(F32) + r.astype(F32) for p, r in zip(self.parts, arrived)]
            n = 2 * tok_rows
            self.parts = [p[:n] for p in sums]
            self.sent = exchange([p[n:].astype(BF16) for p in sums], 0)

        def pair(self, *beside):
            arrived = tied(self.sent, beside)
            sums = [p + r.astype(F32) for p, r in zip(self.parts, arrived)]
            n = tok_rows
            self.parts = jnp.concatenate([p[:n] for p in sums], axis=0)
            self.sent = across(
                jnp.concatenate([p[n:] for p in sums], axis=0).astype(BF16), opening
            )

        def close(self, *beside):
            return self.parts + tied([self.sent], beside)[0].astype(F32)

    flip_b, flip_h, place = [], [], []
    for last in range(2):
        for other in range(2):
            for r, (one, two) in enumerate(orders):
                db, dh = np.array([0, opening[0]]), np.array([0, opening[1]])
                db, dh = np.concatenate([db, db ^ one[0]]), np.concatenate([dh, dh ^ one[1]])
                if last:
                    db, dh = db ^ two[0], dh ^ two[1]
                dh = dh ^ other
                flip_b.append(np.repeat(db, tok_rows) ^ (half if r else 0))
                flip_h.append(np.repeat(dh, tok_rows))
                place.append(np.tile(np.arange(tok_rows), 4))
    flip_b, flip_h, place = (np.concatenate(t).astype(np.int32) for t in (flip_b, flip_h, place))

    def positions(block):
        return ((block ^ flip_b) * nh + (h ^ flip_h)) * tok_rows + place

    pos = positions(b)
    rates = 10000.0 ** (-jnp.arange(HEAD_DIM // 2, dtype=F32) * 2.0 / HEAD_DIM)
    angles = pos.astype(F32)[:, None] * rates[None, :]
    cosine, sine = jnp.cos(angles), jnp.sin(angles)
    table = jnp.concatenate([cosine, cosine, -sine, sine], axis=1)

    def to_micro(pair, *beside):
        keep = jnp.where(second, pair[1], pair[0])
        send = jnp.where(second, pair[0], pair[1])
        arrived = tied([move(send, db=half, dh=0)], beside)[0]
        return jnp.concatenate([keep, arrived], axis=0)

    def from_micro(rows):
        arrived = move(rows[tok_rows:], db=half, dh=0)
        kept = rows[:tok_rows]
        return jnp.stack(
            [jnp.where(second, arrived, kept), jnp.where(second, kept, arrived)]
        )

    alike = [[g * slices + l for g in range(groups)] for l in range(slices)]

    def to_groups(piece):
        return lax.all_gather(piece, "blk", axis=0, tiled=True, axis_index_groups=alike)

    def from_slices(pieces):
        return [move(p, db=d + 1, dh=0) for d, p in enumerate(pieces[1:])]

    def from_groups(grads):
        return lax.psum_scatter(
            grads, "blk", scatter_dimension=0, tiled=True, axis_index_groups=alike
        )

    def collect(whole):
        whole = whole.reshape(slices, kin, -1)
        pick = lambda d: lax.dynamic_index_in_dim(whole, low ^ d, 0, False)
        return [pick(0)] + [move(pick(d), db=d, dh=0) for d in range(1, slices)]

    every = tuple(range(slices))
    attn_own = pack(scalar(low), (w_query, w_key, w_value, w_out), slices, kin)
    feed_own = pack(scalar(low), (w_gate, w_up, w_down), slices, kin)
    tokens = to_micro(block_input, table, *attn_own, *feed_own).astype(F32)
    attn_rest = from_slices(attn_own)
    feed_all = [to_groups(feed_own[0])]
    attn_all = to_groups(
        after(jnp.concatenate([attn_own[0]] + attn_rest, axis=0), *feed_all)
    )
    w_attn = assemble(scalar(low), [(attn_all, every)], kin, slices)
    normed_f, rstd_in = norm_stats(tokens)
    first = Gather(normed_f.astype(BF16))
    first.open(*attn_rest)
    feed_rest = from_slices(feed_own)
    first.take(feed_rest[1])
    normed = first.near + first.far(feed_rest[0], feed_rest[2])
    for piece in (feed_rest[1], feed_rest[0], feed_rest[2]):
        feed_all.append(to_groups(piece))
    back_rows = to_micro(cotangent)
    cots = Gather(after(back_rows, *normed[:2]))
    query, key, value = project(normed, w_attn, table)
    cots.open(query)
    if spread > 1:
        teams = [
            [(((m * spread + s) * slices + l) * nh + k) for s in range(spread)]
            for m in range(2)
            for l in range(slices)
            for k in range(nh)
        ]
        everyone = lambda t: lax.all_gather(t, AXES, axis=0, tiled=True, axis_index_groups=teams)
        keys, values = everyone(key), everyone(value)
        first = b - (group % spread) * slices
        pos_k = jnp.concatenate([positions(first + s * slices) for s in range(spread)])
    else:
        keys, values, pos_k = key, value, pos

    pos_q, pos_k = pos[:, None], pos_k[None, :]
    low1, lse1, kept, sent = attend(query, keys, values, w_attn, pos_q, pos_k, 1)
    mixing = Scatter(kept, sent)
    mixing.open()
    low0, lse0, kept, sent = attend(
        after(query, *mixing.far), keys, values, w_attn, pos_q, pos_k, 0
    )
    mixing.near(kept, sent)
    mixing.take_near()
    mixing.take(feed_all[1])
    cots.take(*mixing.parts)
    mixing.pair()
    mid = tokens + mixing.close(feed_all[2])
    mid_f, rstd_mid = norm_stats(mid)

    mids = Gather(mid_f.astype(BF16))
    mids.open(*cots.sent)
    backs_far = cots.far(*mids.parts)
    backs_near = cots.near
    mids.take(*backs_far, feed_all[3])
    w_feed = assemble(
        scalar(low),
        [(a, d) for a, d in zip(feed_all, ((0,), (2,), (1,), (3,)))],
        kin,
        slices,
    )
    paired0, hidden0, kept0, sent0 = feed(mids.near, backs_near, w_feed)
    mids_far = mids.far(hidden0)
    paired1, hidden1, kept, sent = feed(mids_far, backs_far, w_feed)
    giving = Scatter(kept, sent)
    giving.open()
    giving.near(kept0, sent0)
    feed_grads = weight_grads(
        [
            (mids.near + mids_far, [paired0, after(paired1, *giving.far)]),
            (backs_near + backs_far, [hidden0, hidden1]),
        ],
        width,
    )
    giving.take_near()
    giving.take(feed_grads)
    feed_whole = from_groups(feed_grads)
    out1 = feed_out(after(hidden1, *giving.parts), w_feed)
    giving.pair(*out1)
    out0 = feed_out(after(hidden0, giving.parts), w_feed)
    back_mid_normed = giving.close(*out0)

    back_mid = back_rows.astype(F32) + norm_back(back_mid_normed, mid_f, rstd_mid)
    turned = gather(back_mid.astype(BF16))
    back_attn = turned[0] + turned[1]

    finishing = Scatter(*(after(o, *turned[1][:2]) for o in out1))
    back_attended = back_project(back_attn, w_attn)
    finishing.open(back_attended)
    finishing.near(*out0)
    lse = jnp.concatenate([lse0, lse1], axis=0)
    back_q, back_k, back_v = attend_back(
        query, after(back_attended, *finishing.far), lse, pos_q, keys, values, pos_k
    )
    finishing.take_near(back_q)
    finishing.take()
    if spread > 1:
        shared = lambda t: lax.psum_scatter(
            t, AXES, scatter_dimension=0, tiled=True, axis_index_groups=teams
        )
        back_k, back_v = shared(back_k), shared(back_v)
    joined1, kept, sent = back_input(
        after(back_q, *finishing.parts), back_k, back_v, table, w_attn, 1
    )
    entering = Scatter(kept, sent)
    entering.open()
    finishing.pair(joined1)
    joined0, kept, sent = back_input(
        after(back_q, finishing.parts), back_k, back_v, table, w_attn, 0
    )
    entering.near(kept, sent)
    output = mid + finishing.close(joined0)
    block_output = from_micro(output.astype(BF16))
    attn_grads = weight_grads(
        [(normed, [joined0, joined1]), (back_attn, [low0, low1])], width
    )
    entering.take_near(attn_grads)
    entering.take()
    entering.pair()
    feed_sum = collect(after(feed_whole, entering.parts))
    back_normed = entering.close()
    grad_gate, grad_up, grad_down = unpack(scalar(low), feed_sum, (unit,) * 3)
    attn_sum = collect(after(from_groups(after(attn_grads, feed_whole)), back_normed))
    grad_query, grad_key, grad_value, grad_out = unpack(
        scalar(low), attn_sum, (HEAD_DIM,) * 4
    )
    input_grad = from_micro((back_mid + norm_back(back_normed, normed_f, rstd_in)).astype(BF16))
    return (
        block_output,
        input_grad,
        grad_query,
        grad_key,
        grad_value,
        grad_out,
        grad_gate,
        grad_up,
        grad_down,
    )


def solution(mesh):
    rows = P(None, AXES, None)
    tall, wide = P("blk", "head"), P("head", "blk")
    placed = (rows, rows, tall, tall, tall, wide, tall, tall, wide)
    return jax.shard_map(
        functools.partial(local, mesh.shape["blk"], mesh.shape["head"]),
        mesh=mesh,
        in_specs=placed,
        out_specs=placed,
        check_vma=False,
    )
```

```python
import functools

import jax
import jax.numpy as jnp
import numpy as np
from jax import lax
from jax.experimental import pallas as pl
from jax.experimental.pallas import tpu as pltpu
from jax.sharding import PartitionSpec as P

HEADS = 16
HEAD_DIM = 128
FF = 8192
AXES = ("blk", "head")
SCALE = HEAD_DIM**-0.5
EPS = 1e-05
F32 = jnp.float32
BF16 = jnp.bfloat16
VMEM = pl.BlockSpec(memory_space=pltpu.VMEM)
SMEM = pl.BlockSpec(memory_space=pltpu.SMEM)
NN = (((1,), (0,)), ((), ()))
NT = (((1,), (1,)), ((), ()))
TN = (((0,), (0,)), ((), ()))


def dot(a, b, dims=NN):
    return lax.dot_general(a, b, dims, preferred_element_type=F32)


def shape(rows, columns, kind=BF16):
    return jax.ShapeDtypeStruct((rows, columns), kind)


def call(kernel, outs, name, flops=0, moved=0, grid=None, **more):
    settings = dict(
        out_shape=outs,
        compiler_params=pltpu.CompilerParams(vmem_limit_bytes=56 * 2**20),
        name=name,
    )
    if flops:
        settings["cost_estimate"] = pl.CostEstimate(
            flops=int(flops), bytes_accessed=int(moved), transcendentals=0
        )
    settings.update(more)
    if grid is not None:
        settings["grid"] = grid
    return pl.pallas_call(kernel, **settings)


def swap(value, nb, nh, db, dh):
    pairs = [
        (b * nh + h, (b ^ db) * nh + (h ^ dh)) for b in range(nb) for h in range(nh)
    ]
    return lax.ppermute(value, AXES, pairs)


def norm_stats(values):
    center = values - jnp.mean(values, axis=-1, keepdims=True)
    spread = jnp.mean(center * center, axis=-1, keepdims=True)
    rstd = lax.rsqrt(spread + EPS)
    return center * rstd, rstd


def norm_back(grad, normed, rstd):
    return (
        grad
        - jnp.mean(grad, axis=-1, keepdims=True)
        - normed * jnp.mean(grad * normed, axis=-1, keepdims=True)
    ) * rstd


def turn(values, table, back=False):
    half = HEAD_DIM // 2
    other = jnp.concatenate([values[:, half:], values[:, :half]], axis=1)
    other = other * table[:, HEAD_DIM:]
    return values * table[:, :HEAD_DIM] + (-other if back else other)


def after(value, *others):
    return lax.optimization_barrier((value,) + others)[0]


def pack(low, weights, slices, kin):
    wide = [w.shape[1] // slices for w in weights[:-1]]
    wide.append(weights[-1].shape[0] // slices)
    total = sum(wide)

    def kernel(low_ref, *refs):
        sources, outs = refs[: len(weights)], refs[len(weights) :]
        for d in range(slices):
            at = 0
            which = low_ref[0] ^ d
            for i, (source, w) in enumerate(zip(sources, wide)):
                where = pl.ds(pl.multiple_of(which * w, 128), w)
                if i < len(wide) - 1:
                    outs[d][:, at : at + w] = source[:, where]
                else:
                    outs[d][:, at : at + w] = source[where, :].T
                at += w

    return call(
        kernel,
        [shape(kin, total)] * slices,
        "pack",
        in_specs=[SMEM] + [VMEM] * len(weights),
        out_specs=[VMEM] * slices,
    )(low, *weights)


def assemble(low, pieces, kin, slices):
    groups = pieces[0][0].shape[0] // (kin * len(pieces[0][1]))
    total = pieces[0][0].shape[1]

    def kernel(low_ref, *refs):
        out = refs[-1]
        for (_, which), piece in zip(pieces, refs):
            for g in range(groups):
                for i, d in enumerate(which):
                    block = g * slices + (low_ref[0] ^ d)
                    rows = pl.ds(pl.multiple_of(block * kin, kin), kin)
                    at = (g * len(which) + i) * kin
                    out[rows, :] = piece[at : at + kin, :]

    return call(
        kernel,
        shape(groups * slices * kin, total),
        "assemble",
        in_specs=[SMEM] + [VMEM] * len(pieces),
        out_specs=VMEM,
    )(low, *[p for p, _ in pieces])


def unpack(low, pieces, wide):
    kin, slices = pieces[0].shape[0], len(pieces)

    def kernel(low_ref, *refs):
        sources, outs = refs[:slices], refs[slices:]
        for d in range(slices):
            at = 0
            which = low_ref[0] ^ d
            for i, (out, w) in enumerate(zip(outs, wide)):
                where = pl.ds(pl.multiple_of(which * w, 128), w)
                part = sources[d][:, at : at + w].astype(F32)
                if i < len(wide) - 1:
                    out[:, where] = part
                else:
                    out[where, :] = part.T
                at += w

    outs = [shape(kin, slices * w, F32) for w in wide[:-1]]
    outs.append(shape(slices * wide[-1], kin, F32))
    return call(
        kernel,
        outs,
        "unpack",
        in_specs=[SMEM] + [VMEM] * slices,
        out_specs=[VMEM] * len(wide),
    )(low, *pieces)


def join(refs):
    return jnp.concatenate([r[...] for r in refs], axis=0)


def project(pieces, weights, table):
    section = pieces[0].shape[0] * 2
    sections = len(pieces) // 2
    rows = section * sections

    def kernel(*refs):
        parts, (w, t, q, k, v) = refs[: len(pieces)], refs[len(pieces) :]
        for s in range(sections):
            out = dot(join(parts[2 * s : 2 * s + 2]), w[:, : 3 * HEAD_DIM])
            at = pl.ds(s * section, section)
            angles = t[at, :]
            q[at, :] = turn(out[:, :HEAD_DIM], angles).astype(BF16)
            k[at, :] = turn(out[:, HEAD_DIM : 2 * HEAD_DIM], angles).astype(BF16)
            v[at, :] = out[:, 2 * HEAD_DIM :].astype(BF16)

    width = weights.shape[0]
    return call(
        kernel,
        [shape(rows, HEAD_DIM)] * 3,
        "project",
        6 * rows * width * HEAD_DIM,
        2 * rows * width,
        in_specs=[VMEM] * (len(pieces) + 2),
        out_specs=[VMEM] * 3,
    )(*pieces, weights, table)


def row_block(keys):
    return max(64, 256 * 2048 // keys)


def split_rows(rows, step, width):
    n = rows // 2 // step
    return (
        n,
        [
            pl.BlockSpec((step, width), lambda i: (jnp.minimum(i, n - 1), 0)),
            pl.BlockSpec((step, width), lambda i: (jnp.maximum(i - n, 0), 0)),
        ],
        [shape(rows // 2, width)] * 2,
    )


def put(n, kept, sent, value):
    @pl.when(pl.program_id(0) < n)
    def _():
        kept[...] = value

    @pl.when(pl.program_id(0) >= n)
    def _():
        sent[...] = value


def attend(q, k, v, weights, pos_q, pos_k, half):
    rows, keys, width = q.shape[0] // 2, k.shape[0], weights.shape[0]
    bq = min(rows // 2, row_block(keys))
    first = half * rows // bq
    n, split, shapes = split_rows(rows, bq, width)

    def kernel(q_ref, k_ref, v_ref, w_ref, pq_ref, pk_ref, o_ref, lse_ref, kept, sent):
        scores = dot(q_ref[...], k_ref[...], NT)
        scores = jnp.where(pk_ref[...] <= pq_ref[...], scores * SCALE, -1e30)
        top = jnp.max(scores, axis=-1, keepdims=True)
        probs = jnp.exp(scores - top)
        total = jnp.sum(probs, axis=-1, keepdims=True)
        low = (dot(probs.astype(BF16), v_ref[...]) / total).astype(BF16)
        o_ref[...] = low
        lse_ref[...] = top + jnp.log(total)
        put(n, kept, sent, dot(low, w_ref[:, 3 * HEAD_DIM :], NT).astype(BF16))

    there = lambda w: pl.BlockSpec((bq, w), lambda i: (i + first, 0))
    here = lambda w: pl.BlockSpec((bq, w), lambda i: (i, 0))
    whole = lambda a: pl.BlockSpec(a.shape, lambda i: (0, 0))
    return call(
        kernel,
        [shape(rows, HEAD_DIM), shape(rows, 1, F32)] + shapes,
        "attend",
        4 * rows * keys * HEAD_DIM + 2 * rows * width * HEAD_DIM,
        2 * rows * width,
        grid=(rows // bq,),
        in_specs=[there(HEAD_DIM), whole(k), whole(v), whole(weights), there(1), whole(pos_k)],
        out_specs=[here(HEAD_DIM), here(1)] + split,
    )(q, k, v, weights, pos_q, pos_k)


def feed(tokens, backs, weights):
    rows, width = sum(p.shape[0] for p in tokens), weights.shape[0]
    unit = weights.shape[1] // 3
    count = len(tokens)
    step = min(256, rows // 2)

    def kernel(*refs):
        xs, gs = refs[:count], refs[count : 2 * count]
        w, paired, hidden, kept, sent, x_all, g_all = refs[2 * count :]
        at = 0
        for x, g in zip(xs, gs):
            x_all[at : at + x.shape[0], :] = x[...]
            g_all[at : at + x.shape[0], :] = g[...]
            at += x.shape[0]

        for first, part in ((0, kept), (rows // 2, sent)):

            @pl.loop(0, rows // 2 // step)
            def _(i):
                at = pl.ds(pl.multiple_of(first + i * step, step), step)
                gate_up = dot(x_all[at, :], w[:, : 2 * unit])
                back = dot(g_all[at, :], w[:, 2 * unit :])
                gate, up = gate_up[:, :unit], gate_up[:, unit:]
                sig = 1.0 / (1.0 + jnp.exp(-gate))
                act = gate * sig
                hidden[at, :] = (act * up).astype(BF16)
                paired[at, :unit] = (back * up * sig * (1.0 + gate * (1.0 - sig))).astype(BF16)
                paired[at, unit:] = (back * act).astype(BF16)
                there = pl.ds(pl.multiple_of(i * step, step), step)
                part[there, :] = dot(paired[at, :], w[:, : 2 * unit], NT).astype(BF16)

    return call(
        kernel,
        [shape(rows, 2 * unit), shape(rows, unit)] + [shape(rows // 2, width)] * 2,
        "feed",
        10 * rows * unit * width,
        2 * rows * width,
        in_specs=[VMEM] * (2 * count + 1),
        out_specs=[VMEM] * 4,
        scratch_shapes=[pltpu.VMEM((rows, width), BF16)] * 2,
    )(*tokens, *backs, weights)


def feed_out(hidden, weights):
    rows, unit = hidden.shape
    width = weights.shape[0]
    step = min(256, rows // 2)
    n, split, shapes = split_rows(rows, step, width)

    def kernel(hidden_ref, w_ref, kept, sent):
        put(n, kept, sent, dot(hidden_ref[...], w_ref[:, 2 * unit :], NT).astype(BF16))

    return call(
        kernel,
        shapes,
        "feed_out",
        2 * rows * unit * width,
        2 * rows * width,
        grid=(rows // step,),
        in_specs=[
            pl.BlockSpec((step, unit), lambda i: (i, 0)),
            pl.BlockSpec(weights.shape, lambda i: (0, 0)),
        ],
        out_specs=split,
    )(hidden, weights)


def weight_grads(pairs, width):
    columns = [sides[0].shape[1] for _, sides in pairs]
    total = sum(columns)
    block = 256
    flat = []
    for pieces, sides in pairs:
        flat += list(pieces) + list(sides)

    def kernel(*refs):
        out = refs[-1]
        at, start = 0, 0
        for (pieces, sides), wide in zip(pairs, columns):
            left = join(refs[at : at + len(pieces)])
            at += len(pieces)
            right = join(refs[at : at + len(sides)])
            at += len(sides)
            out[:, start : start + wide] = dot(left, right, TN).astype(BF16)
            start += wide

    specs = []
    for pieces, sides in pairs:
        specs += [pl.BlockSpec((p.shape[0], block), lambda j: (0, j)) for p in pieces]
        specs += [pl.BlockSpec(s.shape, lambda j: (0, 0)) for s in sides]
    rows = sum(p.shape[0] for p in pairs[0][0])
    return call(
        kernel,
        shape(width, total),
        "weight_grads",
        2 * rows * width * total,
        2 * rows * (width + total),
        grid=(width // block,),
        in_specs=specs,
        out_specs=pl.BlockSpec((block, total), lambda j: (j, 0)),
    )(*flat)


def back_project(pieces, weights):
    rows, width = sum(p.shape[0] for p in pieces), weights.shape[0]

    def kernel(*refs):
        w, out = refs[-2:]
        at = 0
        for s in range(len(pieces) // 2):
            x = join(refs[2 * s : 2 * s + 2])
            out[at : at + x.shape[0], :] = dot(x, w[:, 3 * HEAD_DIM :]).astype(BF16)
            at += x.shape[0]

    return call(
        kernel,
        shape(rows, HEAD_DIM),
        "back_project",
        2 * rows * width * HEAD_DIM,
        2 * rows * width,
        in_specs=[VMEM] * (len(pieces) + 1),
        out_specs=VMEM,
    )(*pieces, weights)


def attend_back(q, do, lse, pos_q, k, v, pos_k):
    rows, keys = q.shape[0], k.shape[0]
    bq = min(rows, row_block(keys))

    def kernel(q_ref, do_ref, lse_ref, pq_ref, k_ref, v_ref, pk_ref, dq_ref, dk_ref, dv_ref):
        @pl.when(pl.program_id(0) == 0)
        def _():
            dk_ref[...] = jnp.zeros_like(dk_ref)
            dv_ref[...] = jnp.zeros_like(dv_ref)

        q, k, v, do = q_ref[...], k_ref[...], v_ref[...], do_ref[...]
        scores = dot(q, k, NT)
        probs = jnp.where(
            pk_ref[...] <= pq_ref[...], jnp.exp(scores * SCALE - lse_ref[...]), 0.0
        )
        dots = dot(do, v, NT)
        delta = jnp.sum(probs * dots, axis=-1, keepdims=True)
        back = (probs * (dots - delta)).astype(BF16)
        dq_ref[...] = dot(back, k) * SCALE
        dk_ref[...] += dot(back, q, TN) * SCALE
        dv_ref[...] += dot(probs.astype(BF16), do, TN)

    row = lambda w: pl.BlockSpec((bq, w), lambda i: (i, 0))
    whole = lambda s: pl.BlockSpec(s, lambda i: (0, 0))
    kv = whole((keys, HEAD_DIM))
    return call(
        kernel,
        [shape(rows, HEAD_DIM, F32), shape(keys, HEAD_DIM, F32), shape(keys, HEAD_DIM, F32)],
        "attend_back",
        10 * rows * keys * HEAD_DIM,
        16 * rows * HEAD_DIM,
        grid=(rows // bq,),
        in_specs=[row(HEAD_DIM), row(HEAD_DIM), row(1), row(1), kv, kv, whole((1, keys))],
        out_specs=[row(HEAD_DIM), kv, kv],
    )(q, do, lse, pos_q, k, v, pos_k)


def back_input(dq, dk, dv, table, weights, half):
    rows, width = dq.shape[0] // 2, weights.shape[0]
    step = min(256, rows // 2)
    first = half * rows // step
    n, split, shapes = split_rows(rows, step, width)

    def kernel(dq_ref, dk_ref, dv_ref, t_ref, w_ref, joined, kept, sent):
        joined[:, :HEAD_DIM] = turn(dq_ref[...], t_ref[...], True).astype(BF16)
        joined[:, HEAD_DIM : 2 * HEAD_DIM] = turn(dk_ref[...], t_ref[...], True).astype(BF16)
        joined[:, 2 * HEAD_DIM :] = dv_ref[...].astype(BF16)
        put(n, kept, sent, dot(joined[...], w_ref[:, : 3 * HEAD_DIM], NT).astype(BF16))

    there = lambda w: pl.BlockSpec((step, w), lambda i: (i + first, 0))
    here = lambda w: pl.BlockSpec((step, w), lambda i: (i, 0))
    return call(
        kernel,
        [shape(rows, 3 * HEAD_DIM)] + shapes,
        "back_input",
        6 * rows * width * HEAD_DIM,
        2 * rows * width,
        grid=(rows // step,),
        in_specs=[there(HEAD_DIM)] * 3
        + [there(2 * HEAD_DIM), pl.BlockSpec(weights.shape, lambda i: (0, 0))],
        out_specs=[here(3 * HEAD_DIM)] + split,
    )(dq, dk, dv, table, weights)


def local(nb, nh, block_input, cotangent, w_query, w_key, w_value, w_out, w_gate, w_up, w_down):
    tok_rows, width = block_input.shape[1:]
    slices = HEADS // nh
    half = nb // 2
    groups = nb // slices
    spread = groups // 2
    kin = width // nb
    unit = FF // HEADS
    b, h = lax.axis_index("blk"), lax.axis_index("head")
    low, group = b % slices, b // slices
    second = b >= half
    mine = 2 * tok_rows
    move = functools.partial(swap, nb=nb, nh=nh)
    scalar = lambda v: v.astype(jnp.int32).reshape(1)

    opening, core = (2, 0), (0, 1)
    orders = [((1, 0), (0, 2)), ((0, 2), (1, 0))]

    def exchange(values, step):
        return [move(v, db=o[step][0], dh=o[step][1]) for v, o in zip(values, orders)]

    def across(value, way):
        return move(value, db=way[0], dh=way[1])

    def tied(values, beside):
        return [after(v, *beside) for v in values] if beside else values

    class Gather:
        def __init__(self, value):
            self.parts = value
            self.sent = across(value, opening)

        def open(self, *beside):
            arrived = tied([self.sent], beside)[0]
            n = tok_rows
            self.parts = [
                jnp.concatenate([self.parts[:n], arrived[:n]], axis=0),
                jnp.concatenate([self.parts[n:], arrived[n:]], axis=0),
            ]
            self.sent = exchange(self.parts, 0)

        def take(self, *beside):
            arrived = tied(self.sent, beside)
            self.parts = [jnp.concatenate([p, r], axis=0) for p, r in zip(self.parts, arrived)]
            self.sent = exchange(self.parts, 1)
            self.near = self.parts + [across(p, core) for p in self.parts]

        def far(self, *beside):
            pieces = tied(self.sent, beside)
            return pieces + [across(p, core) for p in pieces]

    def gather(value):
        work = Gather(value)
        work.open()
        work.take()
        return work.near, work.far()

    class Scatter:
        def __init__(self, kept, sent):
            self.kept, self.sent = kept, across(sent, core)

        def add(self, *beside):
            arrived = tied([self.sent], beside)[0]
            n = self.kept.shape[0] // 2
            return [
                (self.kept[r].astype(F32) + arrived[r].astype(F32)).astype(BF16)
                for r in (slice(0, n), slice(n, 2 * n))
            ]

        def open(self, *beside):
            self.far = self.add(*beside)
            self.sent_far = exchange(self.far, 1)

        def near(self, kept, sent):
            self.kept, self.sent = kept, across(sent, core)

        def take_near(self, *beside):
            self.parts = self.add(*beside)

        def take(self, *beside):
            arrived = tied(self.sent_far, beside)
            sums = [p.astype(F32) + r.astype(F32) for p, r in zip(self.parts, arrived)]
            n = 2 * tok_rows
            self.parts = [p[:n] for p in sums]
            self.sent = exchange([p[n:].astype(BF16) for p in sums], 0)

        def pair(self, *beside):
            arrived = tied(self.sent, beside)
            sums = [p + r.astype(F32) for p, r in zip(self.parts, arrived)]
            n = tok_rows
            self.parts = jnp.concatenate([p[:n] for p in sums], axis=0)
            self.sent = across(
                jnp.concatenate([p[n:] for p in sums], axis=0).astype(BF16), opening
            )

        def close(self, *beside):
            return self.parts + tied([self.sent], beside)[0].astype(F32)

    flip_b, flip_h, place = [], [], []
    for last in range(2):
        for other in range(2):
            for r, (one, two) in enumerate(orders):
                db, dh = np.array([0, opening[0]]), np.array([0, opening[1]])
                db, dh = np.concatenate([db, db ^ one[0]]), np.concatenate([dh, dh ^ one[1]])
                if last:
                    db, dh = db ^ two[0], dh ^ two[1]
                dh = dh ^ other
                flip_b.append(np.repeat(db, tok_rows) ^ (half if r else 0))
                flip_h.append(np.repeat(dh, tok_rows))
                place.append(np.tile(np.arange(tok_rows), 4))
    flip_b, flip_h, place = (np.concatenate(t).astype(np.int32) for t in (flip_b, flip_h, place))

    def positions(block):
        return ((block ^ flip_b) * nh + (h ^ flip_h)) * tok_rows + place

    pos = positions(b)
    rates = 10000.0 ** (-jnp.arange(HEAD_DIM // 2, dtype=F32) * 2.0 / HEAD_DIM)
    angles = pos.astype(F32)[:, None] * rates[None, :]
    cosine, sine = jnp.cos(angles), jnp.sin(angles)
    table = jnp.concatenate([cosine, cosine, -sine, sine], axis=1)

    def to_micro(pair, *beside):
        keep = jnp.where(second, pair[1], pair[0])
        send = jnp.where(second, pair[0], pair[1])
        arrived = tied([move(send, db=half, dh=0)], beside)[0]
        return jnp.concatenate([keep, arrived], axis=0)

    def from_micro(rows):
        arrived = move(rows[tok_rows:], db=half, dh=0)
        kept = rows[:tok_rows]
        return jnp.stack(
            [jnp.where(second, arrived, kept), jnp.where(second, kept, arrived)]
        )

    alike = [[g * slices + l for g in range(groups)] for l in range(slices)]

    def to_groups(piece):
        return lax.all_gather(piece, "blk", axis=0, tiled=True, axis_index_groups=alike)

    def doubled(piece):
        step = slices
        while step < nb:
            arrived = move(piece, db=step, dh=0)
            upper = (b // step) % 2 == 1
            piece = jnp.where(
                upper,
                jnp.concatenate([arrived, piece], axis=0),
                jnp.concatenate([piece, arrived], axis=0),
            )
            step *= 2
        return piece

    def from_slices(pieces):
        return [move(p, db=d + 1, dh=0) for d, p in enumerate(pieces[1:])]

    def from_groups(grads):
        return lax.psum_scatter(
            grads, "blk", scatter_dimension=0, tiled=True, axis_index_groups=alike
        )

    def collect(whole):
        whole = whole.reshape(slices, kin, -1)
        pick = lambda d: lax.dynamic_index_in_dim(whole, low ^ d, 0, False)
        return [pick(0)] + [move(pick(d), db=d, dh=0) for d in range(1, slices)]

    every = tuple(range(slices))
    attn_own = pack(scalar(low), (w_query, w_key, w_value, w_out), slices, kin)
    feed_own = pack(scalar(low), (w_gate, w_up, w_down), slices, kin)
    tokens = to_micro(block_input, table, *attn_own, *feed_own).astype(F32)
    attn_rest = from_slices(attn_own)
    feed_all = [to_groups(feed_own[0])]
    attn_all = to_groups(
        after(jnp.concatenate([attn_own[0]] + attn_rest, axis=0), *feed_all)
    )
    w_attn = assemble(scalar(low), [(attn_all, every)], kin, slices)
    normed_f, rstd_in = norm_stats(tokens)
    first = Gather(normed_f.astype(BF16))
    back_rows = to_micro(cotangent)
    first.open(*attn_rest, back_rows)
    feed_rest = from_slices(feed_own)
    first.take()
    normed = first.near + first.far(*feed_rest)
    for piece in (feed_rest[1], feed_rest[0]):
        feed_all.append(to_groups(piece))
    feed_all.append(doubled(feed_rest[2]))
    cots = Gather(after(back_rows, *normed[:2]))
    query, key, value = project(normed, w_attn, table)
    if spread > 1:
        teams = [
            [(((m * spread + s) * slices + l) * nh + k) for s in range(spread)]
            for m in range(2)
            for l in range(slices)
            for k in range(nh)
        ]
        everyone = lambda t: lax.all_gather(t, AXES, axis=0, tiled=True, axis_index_groups=teams)
        keys, values = everyone(key), everyone(value)
        first = b - (group % spread) * slices
        pos_k = jnp.concatenate([positions(first + s * slices) for s in range(spread)])
    else:
        keys, values, pos_k = key, value, pos

    pos_q, pos_k = pos[:, None], pos_k[None, :]
    low1, lse1, kept, sent = attend(query, keys, values, w_attn, pos_q, pos_k, 1)
    mixing = Scatter(kept, sent)
    mixing.open()
    low0, lse0, kept, sent = attend(
        after(query, *mixing.far, cots.sent), keys, values, w_attn, pos_q, pos_k, 0
    )
    cots.open()
    mixing.near(kept, sent)
    mixing.take_near()
    mixing.take(feed_all[1])
    cots.take(*mixing.parts)
    mixing.pair()
    mid = tokens + mixing.close(feed_all[2], feed_all[3])
    mid_f, rstd_mid = norm_stats(mid)

    mids = Gather(mid_f.astype(BF16))
    mids.open(*cots.sent)
    backs_far = cots.far(*mids.parts)
    backs_near = cots.near
    mids.take(*backs_far)
    w_feed = assemble(
        scalar(low),
        [(a, d) for a, d in zip(feed_all, ((0,), (2,), (1,), (3,)))],
        kin,
        slices,
    )
    paired0, hidden0, kept0, sent0 = feed(mids.near, backs_near, w_feed)
    mids_far = mids.far(hidden0)
    paired1, hidden1, kept, sent = feed(mids_far, backs_far, w_feed)
    giving = Scatter(kept, sent)
    giving.open()
    giving.near(kept0, sent0)
    feed_grads = weight_grads(
        [
            (mids.near + mids_far, [paired0, after(paired1, *giving.far)]),
            (backs_near + backs_far, [hidden0, hidden1]),
        ],
        width,
    )
    giving.take_near()
    giving.take(feed_grads)
    feed_whole = from_groups(feed_grads)
    out1 = feed_out(after(hidden1, *giving.parts), w_feed)
    giving.pair(*out1)
    out0 = feed_out(after(hidden0, giving.parts), w_feed)
    back_mid_normed = giving.close(*out0)

    back_mid = back_rows.astype(F32) + norm_back(back_mid_normed, mid_f, rstd_mid)
    turned = gather(back_mid.astype(BF16))
    back_attn = turned[0] + turned[1]

    finishing = Scatter(*(after(o, *turned[1][:2]) for o in out1))
    back_attended = back_project(back_attn, w_attn)
    finishing.open(back_attended)
    finishing.near(*out0)
    lse = jnp.concatenate([lse0, lse1], axis=0)
    back_q, back_k, back_v = attend_back(
        query, after(back_attended, *finishing.far), lse, pos_q, keys, values, pos_k
    )
    finishing.take_near(back_q)
    finishing.take()
    if spread > 1:
        shared = lambda t: lax.psum_scatter(
            t, AXES, scatter_dimension=0, tiled=True, axis_index_groups=teams
        )
        back_k, back_v = shared(back_k), shared(back_v)
    joined1, kept, sent = back_input(
        after(back_q, *finishing.sent_far), back_k, back_v, table, w_attn, 1
    )
    entering = Scatter(kept, sent)
    entering.open()
    finishing.pair(joined1)
    joined0, kept, sent = back_input(
        after(back_q, finishing.parts), back_k, back_v, table, w_attn, 0
    )
    entering.near(kept, sent)
    output = mid + finishing.close(joined0)
    block_output = from_micro(output.astype(BF16))
    attn_grads = weight_grads(
        [(normed, [joined0, joined1]), (back_attn, [low0, low1])], width
    )
    entering.take_near(attn_grads)
    entering.take()
    entering.pair()
    feed_sum = collect(after(feed_whole, entering.parts))
    back_normed = entering.close()
    grad_gate, grad_up, grad_down = unpack(scalar(low), feed_sum, (unit,) * 3)
    attn_sum = collect(after(from_groups(after(attn_grads, feed_whole)), back_normed))
    grad_query, grad_key, grad_value, grad_out = unpack(
        scalar(low), attn_sum, (HEAD_DIM,) * 4
    )
    input_grad = from_micro((back_mid + norm_back(back_normed, normed_f, rstd_in)).astype(BF16))
    return (
        block_output,
        input_grad,
        grad_query,
        grad_key,
        grad_value,
        grad_out,
        grad_gate,
        grad_up,
        grad_down,
    )


def solution(mesh):
    rows = P(None, AXES, None)
    tall, wide = P("blk", "head"), P("head", "blk")
    placed = (rows, rows, tall, tall, tall, wide, tall, tall, wide)
    return jax.shard_map(
        functools.partial(local, mesh.shape["blk"], mesh.shape["head"]),
        mesh=mesh,
        in_specs=placed,
        out_specs=placed,
        check_vma=False,
    )
```

```python
import functools

import jax
import jax.numpy as jnp
import numpy as np
from jax import lax
from jax.experimental import pallas as pl
from jax.experimental.pallas import tpu as pltpu
from jax.sharding import PartitionSpec as P

HEADS = 16
HEAD_DIM = 128
FF = 8192
AXES = ("blk", "head")
SCALE = HEAD_DIM**-0.5
EPS = 1e-05
F32 = jnp.float32
BF16 = jnp.bfloat16
VMEM = pl.BlockSpec(memory_space=pltpu.VMEM)
SMEM = pl.BlockSpec(memory_space=pltpu.SMEM)
NN = (((1,), (0,)), ((), ()))
NT = (((1,), (1,)), ((), ()))
TN = (((0,), (0,)), ((), ()))


def dot(a, b, dims=NN):
    return lax.dot_general(a, b, dims, preferred_element_type=F32)


def shape(rows, columns, kind=BF16):
    return jax.ShapeDtypeStruct((rows, columns), kind)


def call(kernel, outs, name, flops=0, moved=0, grid=None, **more):
    settings = dict(
        out_shape=outs,
        compiler_params=pltpu.CompilerParams(vmem_limit_bytes=56 * 2**20),
        name=name,
    )
    if flops:
        settings["cost_estimate"] = pl.CostEstimate(
            flops=int(flops), bytes_accessed=int(moved), transcendentals=0
        )
    settings.update(more)
    if grid is not None:
        settings["grid"] = grid
    return pl.pallas_call(kernel, **settings)


def swap(value, nb, nh, db, dh):
    pairs = [
        (b * nh + h, (b ^ db) * nh + (h ^ dh)) for b in range(nb) for h in range(nh)
    ]
    return lax.ppermute(value, AXES, pairs)


def norm_stats(values):
    center = values - jnp.mean(values, axis=-1, keepdims=True)
    spread = jnp.mean(center * center, axis=-1, keepdims=True)
    rstd = lax.rsqrt(spread + EPS)
    return center * rstd, rstd


def norm_back(grad, normed, rstd):
    return (
        grad
        - jnp.mean(grad, axis=-1, keepdims=True)
        - normed * jnp.mean(grad * normed, axis=-1, keepdims=True)
    ) * rstd


def turn(values, table, back=False):
    half = HEAD_DIM // 2
    other = jnp.concatenate([values[:, half:], values[:, :half]], axis=1)
    other = other * table[:, HEAD_DIM:]
    return values * table[:, :HEAD_DIM] + (-other if back else other)


def after(value, *others):
    return lax.optimization_barrier((value,) + others)[0]


def pack(low, weights, slices, kin):
    wide = [w.shape[1] // slices for w in weights[:-1]]
    wide.append(weights[-1].shape[0] // slices)
    total = sum(wide)

    def kernel(low_ref, *refs):
        sources, outs = refs[: len(weights)], refs[len(weights) :]
        for d in range(slices):
            at = 0
            which = low_ref[0] ^ d
            for i, (source, w) in enumerate(zip(sources, wide)):
                where = pl.ds(pl.multiple_of(which * w, 128), w)
                if i < len(wide) - 1:
                    outs[d][:, at : at + w] = source[:, where]
                else:
                    outs[d][:, at : at + w] = source[where, :].T
                at += w

    return call(
        kernel,
        [shape(kin, total)] * slices,
        "pack",
        in_specs=[SMEM] + [VMEM] * len(weights),
        out_specs=[VMEM] * slices,
    )(low, *weights)


def assemble(low, pieces, kin, slices):
    groups = pieces[0][0].shape[0] // (kin * len(pieces[0][1]))
    total = pieces[0][0].shape[1]

    def kernel(low_ref, *refs):
        out = refs[-1]
        for (_, which), piece in zip(pieces, refs):
            for g in range(groups):
                for i, d in enumerate(which):
                    block = g * slices + (low_ref[0] ^ d)
                    rows = pl.ds(pl.multiple_of(block * kin, kin), kin)
                    at = (g * len(which) + i) * kin
                    out[rows, :] = piece[at : at + kin, :]

    return call(
        kernel,
        shape(groups * slices * kin, total),
        "assemble",
        in_specs=[SMEM] + [VMEM] * len(pieces),
        out_specs=VMEM,
    )(low, *[p for p, _ in pieces])


def unpack(low, pieces, wide):
    kin, slices = pieces[0].shape[0], len(pieces)

    def kernel(low_ref, *refs):
        sources, outs = refs[:slices], refs[slices:]
        for d in range(slices):
            at = 0
            which = low_ref[0] ^ d
            for i, (out, w) in enumerate(zip(outs, wide)):
                where = pl.ds(pl.multiple_of(which * w, 128), w)
                part = sources[d][:, at : at + w].astype(F32)
                if i < len(wide) - 1:
                    out[:, where] = part
                else:
                    out[where, :] = part.T
                at += w

    outs = [shape(kin, slices * w, F32) for w in wide[:-1]]
    outs.append(shape(slices * wide[-1], kin, F32))
    return call(
        kernel,
        outs,
        "unpack",
        in_specs=[SMEM] + [VMEM] * slices,
        out_specs=[VMEM] * len(wide),
    )(low, *pieces)


def join(refs):
    return jnp.concatenate([r[...] for r in refs], axis=0)


def project(pieces, weights, table):
    section = pieces[0].shape[0] * 2
    sections = len(pieces) // 2
    rows = section * sections

    def kernel(*refs):
        parts, (w, t, q, k, v) = refs[: len(pieces)], refs[len(pieces) :]
        for s in range(sections):
            out = dot(join(parts[2 * s : 2 * s + 2]), w[:, : 3 * HEAD_DIM])
            at = pl.ds(s * section, section)
            angles = t[at, :]
            q[at, :] = turn(out[:, :HEAD_DIM], angles).astype(BF16)
            k[at, :] = turn(out[:, HEAD_DIM : 2 * HEAD_DIM], angles).astype(BF16)
            v[at, :] = out[:, 2 * HEAD_DIM :].astype(BF16)

    width = weights.shape[0]
    return call(
        kernel,
        [shape(rows, HEAD_DIM)] * 3,
        "project",
        6 * rows * width * HEAD_DIM,
        2 * rows * width,
        in_specs=[VMEM] * (len(pieces) + 2),
        out_specs=[VMEM] * 3,
    )(*pieces, weights, table)


def row_block(keys, rows):
    return max(64, rows * 2048 // keys)


def split_rows(rows, step, width):
    n = rows // 2 // step
    return (
        n,
        [
            pl.BlockSpec((step, width), lambda i: (jnp.minimum(i, n - 1), 0)),
            pl.BlockSpec((step, width), lambda i: (jnp.maximum(i - n, 0), 0)),
        ],
        [shape(rows // 2, width)] * 2,
    )


def put(n, kept, sent, value):
    @pl.when(pl.program_id(0) < n)
    def _():
        kept[...] = value

    @pl.when(pl.program_id(0) >= n)
    def _():
        sent[...] = value


def attend(q, k, v, weights, pos_q, pos_k, half):
    rows, keys, width = q.shape[0] // 2, k.shape[0], weights.shape[0]
    bq = min(rows // 2, row_block(keys, 256))
    first = half * rows // bq
    n, split, shapes = split_rows(rows, bq, width)

    def kernel(q_ref, k_ref, v_ref, w_ref, pq_ref, pk_ref, o_ref, lse_ref, kept, sent):
        scores = dot(q_ref[...], k_ref[...], NT)
        scores = jnp.where(pk_ref[...] <= pq_ref[...], scores * SCALE, -1e30)
        top = jnp.max(scores, axis=-1, keepdims=True)
        probs = jnp.exp(scores - top)
        total = jnp.sum(probs, axis=-1, keepdims=True)
        low = (dot(probs.astype(BF16), v_ref[...]) / total).astype(BF16)
        o_ref[...] = low
        lse_ref[...] = top + jnp.log(total)
        put(n, kept, sent, dot(low, w_ref[:, 3 * HEAD_DIM :], NT).astype(BF16))

    there = lambda w: pl.BlockSpec((bq, w), lambda i: (i + first, 0))
    here = lambda w: pl.BlockSpec((bq, w), lambda i: (i, 0))
    whole = lambda a: pl.BlockSpec(a.shape, lambda i: (0, 0))
    return call(
        kernel,
        [shape(rows, HEAD_DIM), shape(rows, 1, F32)] + shapes,
        "attend",
        4 * rows * keys * HEAD_DIM + 2 * rows * width * HEAD_DIM,
        2 * rows * width,
        grid=(rows // bq,),
        in_specs=[there(HEAD_DIM), whole(k), whole(v), whole(weights), there(1), whole(pos_k)],
        out_specs=[here(HEAD_DIM), here(1)] + split,
    )(q, k, v, weights, pos_q, pos_k)


def feed(tokens, backs, weights):
    rows, width = sum(p.shape[0] for p in tokens), weights.shape[0]
    unit = weights.shape[1] // 3
    count = len(tokens)
    step = min(512, rows // 2)

    def kernel(*refs):
        xs, gs = refs[:count], refs[count : 2 * count]
        w, paired, hidden, kept, sent, x_all, g_all = refs[2 * count :]
        at = 0
        for x, g in zip(xs, gs):
            x_all[at : at + x.shape[0], :] = x[...]
            g_all[at : at + x.shape[0], :] = g[...]
            at += x.shape[0]

        for first, part in ((0, kept), (rows // 2, sent)):

            @pl.loop(0, rows // 2 // step)
            def _(i):
                at = pl.ds(pl.multiple_of(first + i * step, step), step)
                gate_up = dot(x_all[at, :], w[:, : 2 * unit])
                back = dot(g_all[at, :], w[:, 2 * unit :])
                gate, up = gate_up[:, :unit], gate_up[:, unit:]
                sig = 1.0 / (1.0 + jnp.exp(-gate))
                act = gate * sig
                hidden[at, :] = (act * up).astype(BF16)
                paired[at, :unit] = (back * up * sig * (1.0 + gate * (1.0 - sig))).astype(BF16)
                paired[at, unit:] = (back * act).astype(BF16)
                there = pl.ds(pl.multiple_of(i * step, step), step)
                part[there, :] = dot(paired[at, :], w[:, : 2 * unit], NT).astype(BF16)

    return call(
        kernel,
        [shape(rows, 2 * unit), shape(rows, unit)] + [shape(rows // 2, width)] * 2,
        "feed",
        10 * rows * unit * width,
        2 * rows * width,
        in_specs=[VMEM] * (2 * count + 1),
        out_specs=[VMEM] * 4,
        scratch_shapes=[pltpu.VMEM((rows, width), BF16)] * 2,
    )(*tokens, *backs, weights)


def feed_out(hidden, weights):
    rows, unit = hidden.shape
    width = weights.shape[0]
    step = min(256, rows // 2)
    n, split, shapes = split_rows(rows, step, width)

    def kernel(hidden_ref, w_ref, kept, sent):
        put(n, kept, sent, dot(hidden_ref[...], w_ref[:, 2 * unit :], NT).astype(BF16))

    return call(
        kernel,
        shapes,
        "feed_out",
        2 * rows * unit * width,
        2 * rows * width,
        grid=(rows // step,),
        in_specs=[
            pl.BlockSpec((step, unit), lambda i: (i, 0)),
            pl.BlockSpec(weights.shape, lambda i: (0, 0)),
        ],
        out_specs=split,
    )(hidden, weights)


def weight_grads(pairs, width):
    columns = [sides[0].shape[1] for _, sides in pairs]
    total = sum(columns)
    block = 512
    flat = []
    for pieces, sides in pairs:
        flat += list(pieces) + list(sides)

    def kernel(*refs):
        out = refs[-1]
        at, start = 0, 0
        for (pieces, sides), wide in zip(pairs, columns):
            left = join(refs[at : at + len(pieces)])
            at += len(pieces)
            right = join(refs[at : at + len(sides)])
            at += len(sides)
            out[:, start : start + wide] = dot(left, right, TN).astype(BF16)
            start += wide

    specs = []
    for pieces, sides in pairs:
        specs += [pl.BlockSpec((p.shape[0], block), lambda j: (0, j)) for p in pieces]
        specs += [pl.BlockSpec(s.shape, lambda j: (0, 0)) for s in sides]
    rows = sum(p.shape[0] for p in pairs[0][0])
    return call(
        kernel,
        shape(width, total),
        "weight_grads",
        2 * rows * width * total,
        2 * rows * (width + total),
        grid=(width // block,),
        in_specs=specs,
        out_specs=pl.BlockSpec((block, total), lambda j: (j, 0)),
    )(*flat)


def back_project(pieces, weights):
    rows, width = sum(p.shape[0] for p in pieces), weights.shape[0]

    def kernel(*refs):
        w, out = refs[-2:]
        at = 0
        for s in range(len(pieces) // 2):
            x = join(refs[2 * s : 2 * s + 2])
            out[at : at + x.shape[0], :] = dot(x, w[:, 3 * HEAD_DIM :]).astype(BF16)
            at += x.shape[0]

    return call(
        kernel,
        shape(rows, HEAD_DIM),
        "back_project",
        2 * rows * width * HEAD_DIM,
        2 * rows * width,
        in_specs=[VMEM] * (len(pieces) + 1),
        out_specs=VMEM,
    )(*pieces, weights)


def attend_back(q, do, lse, pos_q, k, v, pos_k):
    rows, keys = q.shape[0], k.shape[0]
    bq = min(rows, row_block(keys, 512))

    def kernel(q_ref, do_ref, lse_ref, pq_ref, k_ref, v_ref, pk_ref, dq_ref, dk_ref, dv_ref):
        @pl.when(pl.program_id(0) == 0)
        def _():
            dk_ref[...] = jnp.zeros_like(dk_ref)
            dv_ref[...] = jnp.zeros_like(dv_ref)

        q, k, v, do = q_ref[...], k_ref[...], v_ref[...], do_ref[...]
        scores = dot(q, k, NT)
        probs = jnp.where(
            pk_ref[...] <= pq_ref[...], jnp.exp(scores * SCALE - lse_ref[...]), 0.0
        )
        dots = dot(do, v, NT)
        delta = jnp.sum(probs * dots, axis=-1, keepdims=True)
        back = (probs * (dots - delta)).astype(BF16)
        dq_ref[...] = dot(back, k) * SCALE
        dk_ref[...] += dot(back, q, TN) * SCALE
        dv_ref[...] += dot(probs.astype(BF16), do, TN)

    row = lambda w: pl.BlockSpec((bq, w), lambda i: (i, 0))
    whole = lambda s: pl.BlockSpec(s, lambda i: (0, 0))
    kv = whole((keys, HEAD_DIM))
    return call(
        kernel,
        [shape(rows, HEAD_DIM, F32), shape(keys, HEAD_DIM, F32), shape(keys, HEAD_DIM, F32)],
        "attend_back",
        10 * rows * keys * HEAD_DIM,
        16 * rows * HEAD_DIM,
        grid=(rows // bq,),
        in_specs=[row(HEAD_DIM), row(HEAD_DIM), row(1), row(1), kv, kv, whole((1, keys))],
        out_specs=[row(HEAD_DIM), kv, kv],
    )(q, do, lse, pos_q, k, v, pos_k)


def back_input(dq, dk, dv, table, weights, half):
    rows, width = dq.shape[0] // 2, weights.shape[0]
    step = min(256, rows // 2)
    first = half * rows // step
    n, split, shapes = split_rows(rows, step, width)

    def kernel(dq_ref, dk_ref, dv_ref, t_ref, w_ref, joined, kept, sent):
        joined[:, :HEAD_DIM] = turn(dq_ref[...], t_ref[...], True).astype(BF16)
        joined[:, HEAD_DIM : 2 * HEAD_DIM] = turn(dk_ref[...], t_ref[...], True).astype(BF16)
        joined[:, 2 * HEAD_DIM :] = dv_ref[...].astype(BF16)
        put(n, kept, sent, dot(joined[...], w_ref[:, : 3 * HEAD_DIM], NT).astype(BF16))

    there = lambda w: pl.BlockSpec((step, w), lambda i: (i + first, 0))
    here = lambda w: pl.BlockSpec((step, w), lambda i: (i, 0))
    return call(
        kernel,
        [shape(rows, 3 * HEAD_DIM)] + shapes,
        "back_input",
        6 * rows * width * HEAD_DIM,
        2 * rows * width,
        grid=(rows // step,),
        in_specs=[there(HEAD_DIM)] * 3
        + [there(2 * HEAD_DIM), pl.BlockSpec(weights.shape, lambda i: (0, 0))],
        out_specs=[here(3 * HEAD_DIM)] + split,
    )(dq, dk, dv, table, weights)


def local(nb, nh, block_input, cotangent, w_query, w_key, w_value, w_out, w_gate, w_up, w_down):
    tok_rows, width = block_input.shape[1:]
    slices = HEADS // nh
    half = nb // 2
    groups = nb // slices
    spread = groups // 2
    kin = width // nb
    unit = FF // HEADS
    b, h = lax.axis_index("blk"), lax.axis_index("head")
    low, group = b % slices, b // slices
    second = b >= half
    mine = 2 * tok_rows
    move = functools.partial(swap, nb=nb, nh=nh)
    scalar = lambda v: v.astype(jnp.int32).reshape(1)

    opening, core = (2, 0), (0, 1)
    orders = [((1, 0), (0, 2)), ((0, 2), (1, 0))]

    def exchange(values, step):
        return [move(v, db=o[step][0], dh=o[step][1]) for v, o in zip(values, orders)]

    def across(value, way):
        return move(value, db=way[0], dh=way[1])

    def tied(values, beside):
        return [after(v, *beside) for v in values] if beside else values

    class Gather:
        def __init__(self, value):
            self.parts = value
            self.sent = across(value, opening)

        def open(self, *beside):
            arrived = tied([self.sent], beside)[0]
            n = tok_rows
            self.parts = [
                jnp.concatenate([self.parts[:n], arrived[:n]], axis=0),
                jnp.concatenate([self.parts[n:], arrived[n:]], axis=0),
            ]
            self.sent = exchange(self.parts, 0)

        def take(self, *beside):
            arrived = tied(self.sent, beside)
            self.parts = [jnp.concatenate([p, r], axis=0) for p, r in zip(self.parts, arrived)]
            self.sent = exchange(self.parts, 1)
            self.near = self.parts + [across(p, core) for p in self.parts]

        def far(self, *beside):
            pieces = tied(self.sent, beside)
            return pieces + [across(p, core) for p in pieces]

    def gather(value):
        work = Gather(value)
        work.open()
        work.take()
        return work.near, work.far()

    class Scatter:
        def __init__(self, kept, sent):
            self.kept, self.sent = kept, across(sent, core)

        def add(self, *beside):
            arrived = tied([self.sent], beside)[0]
            n = self.kept.shape[0] // 2
            return [
                (self.kept[r].astype(F32) + arrived[r].astype(F32)).astype(BF16)
                for r in (slice(0, n), slice(n, 2 * n))
            ]

        def open(self, *beside):
            self.far = self.add(*beside)
            self.sent_far = exchange(self.far, 1)

        def near(self, kept, sent):
            self.kept, self.sent = kept, across(sent, core)

        def take_near(self, *beside):
            self.parts = self.add(*beside)

        def take(self, *beside):
            arrived = tied(self.sent_far, beside)
            sums = [p.astype(F32) + r.astype(F32) for p, r in zip(self.parts, arrived)]
            n = 2 * tok_rows
            self.parts = [p[:n] for p in sums]
            self.sent = exchange([p[n:].astype(BF16) for p in sums], 0)

        def pair(self, *beside):
            arrived = tied(self.sent, beside)
            sums = [p + r.astype(F32) for p, r in zip(self.parts, arrived)]
            n = tok_rows
            self.parts = jnp.concatenate([p[:n] for p in sums], axis=0)
            self.sent = across(
                jnp.concatenate([p[n:] for p in sums], axis=0).astype(BF16), opening
            )

        def close(self, *beside):
            return self.parts + tied([self.sent], beside)[0].astype(F32)

    flip_b, flip_h, place = [], [], []
    for last in range(2):
        for other in range(2):
            for r, (one, two) in enumerate(orders):
                db, dh = np.array([0, opening[0]]), np.array([0, opening[1]])
                db, dh = np.concatenate([db, db ^ one[0]]), np.concatenate([dh, dh ^ one[1]])
                if last:
                    db, dh = db ^ two[0], dh ^ two[1]
                dh = dh ^ other
                flip_b.append(np.repeat(db, tok_rows) ^ (half if r else 0))
                flip_h.append(np.repeat(dh, tok_rows))
                place.append(np.tile(np.arange(tok_rows), 4))
    flip_b, flip_h, place = (np.concatenate(t).astype(np.int32) for t in (flip_b, flip_h, place))

    def positions(block):
        return ((block ^ flip_b) * nh + (h ^ flip_h)) * tok_rows + place

    pos = positions(b)
    rates = 10000.0 ** (-jnp.arange(HEAD_DIM // 2, dtype=F32) * 2.0 / HEAD_DIM)
    angles = pos.astype(F32)[:, None] * rates[None, :]
    cosine, sine = jnp.cos(angles), jnp.sin(angles)
    table = jnp.concatenate([cosine, cosine, -sine, sine], axis=1)

    def to_micro(pair, *beside):
        keep = jnp.where(second, pair[1], pair[0])
        send = jnp.where(second, pair[0], pair[1])
        arrived = tied([move(send, db=half, dh=0)], beside)[0]
        return jnp.concatenate([keep, arrived], axis=0)

    def from_micro(rows):
        arrived = move(rows[tok_rows:], db=half, dh=0)
        kept = rows[:tok_rows]
        return jnp.stack(
            [jnp.where(second, arrived, kept), jnp.where(second, kept, arrived)]
        )

    alike = [[g * slices + l for g in range(groups)] for l in range(slices)]

    def to_groups(piece):
        return lax.all_gather(piece, "blk", axis=0, tiled=True, axis_index_groups=alike)

    def doubled(piece):
        step = slices
        while step < nb:
            arrived = move(piece, db=step, dh=0)
            upper = (b // step) % 2 == 1
            piece = jnp.where(
                upper,
                jnp.concatenate([arrived, piece], axis=0),
                jnp.concatenate([piece, arrived], axis=0),
            )
            step *= 2
        return piece

    def from_slices(pieces):
        return [move(p, db=d + 1, dh=0) for d, p in enumerate(pieces[1:])]

    def from_groups(grads):
        return lax.psum_scatter(
            grads, "blk", scatter_dimension=0, tiled=True, axis_index_groups=alike
        )

    def collect(whole):
        whole = whole.reshape(slices, kin, -1)
        pick = lambda d: lax.dynamic_index_in_dim(whole, low ^ d, 0, False)
        return [pick(0)] + [move(pick(d), db=d, dh=0) for d in range(1, slices)]

    every = tuple(range(slices))
    attn_own = pack(scalar(low), (w_query, w_key, w_value, w_out), slices, kin)
    feed_own = pack(scalar(low), (w_gate, w_up, w_down), slices, kin)
    tokens = to_micro(block_input, table, *attn_own, *feed_own).astype(F32)
    attn_rest = from_slices(attn_own)
    feed_all = [to_groups(feed_own[0])]
    attn_all = to_groups(
        after(jnp.concatenate([attn_own[0]] + attn_rest, axis=0), *feed_all)
    )
    w_attn = assemble(scalar(low), [(attn_all, every)], kin, slices)
    normed_f, rstd_in = norm_stats(tokens)
    first = Gather(normed_f.astype(BF16))
    back_rows = to_micro(cotangent)
    first.open(*attn_rest, back_rows)
    feed_rest = from_slices(feed_own)
    first.take()
    normed = first.near + first.far(*feed_rest)
    for piece in (feed_rest[1], feed_rest[0]):
        feed_all.append(to_groups(piece))
    feed_all.append(doubled(feed_rest[2]))
    cots = Gather(after(back_rows, *normed[:2]))
    query, key, value = project(normed, w_attn, table)
    if spread > 1:
        teams = [
            [(((m * spread + s) * slices + l) * nh + k) for s in range(spread)]
            for m in range(2)
            for l in range(slices)
            for k in range(nh)
        ]
        everyone = lambda t: lax.all_gather(t, AXES, axis=0, tiled=True, axis_index_groups=teams)
        keys, values = everyone(key), everyone(value)
        first = b - (group % spread) * slices
        pos_k = jnp.concatenate([positions(first + s * slices) for s in range(spread)])
    else:
        keys, values, pos_k = key, value, pos

    pos_q, pos_k = pos[:, None], pos_k[None, :]
    low1, lse1, kept, sent = attend(query, keys, values, w_attn, pos_q, pos_k, 1)
    mixing = Scatter(kept, sent)
    mixing.open()
    low0, lse0, kept, sent = attend(
        after(query, *mixing.far, cots.sent), keys, values, w_attn, pos_q, pos_k, 0
    )
    cots.open()
    mixing.near(kept, sent)
    mixing.take_near()
    mixing.take(feed_all[1])
    cots.take(*mixing.parts)
    mixing.pair()
    mid = tokens + mixing.close(feed_all[2], feed_all[3])
    mid_f, rstd_mid = norm_stats(mid)

    mids = Gather(mid_f.astype(BF16))
    mids.open(*cots.sent)
    backs_far = cots.far(*mids.parts)
    backs_near = cots.near
    mids.take(*backs_far)
    w_feed = assemble(
        scalar(low),
        [(a, d) for a, d in zip(feed_all, ((0,), (2,), (1,), (3,)))],
        kin,
        slices,
    )
    paired0, hidden0, kept0, sent0 = feed(mids.near, backs_near, w_feed)
    mids_far = mids.far(hidden0)
    paired1, hidden1, kept, sent = feed(mids_far, backs_far, w_feed)
    giving = Scatter(kept, sent)
    giving.open()
    giving.near(kept0, sent0)
    feed_grads = weight_grads(
        [
            (mids.near + mids_far, [paired0, after(paired1, *giving.far)]),
            (backs_near + backs_far, [hidden0, hidden1]),
        ],
        width,
    )
    giving.take_near()
    giving.take(feed_grads)
    feed_whole = from_groups(feed_grads)
    out1 = feed_out(after(hidden1, *giving.parts), w_feed)
    giving.pair(*out1)
    out0 = feed_out(after(hidden0, giving.parts), w_feed)
    back_mid_normed = giving.close(*out0)

    back_mid = back_rows.astype(F32) + norm_back(back_mid_normed, mid_f, rstd_mid)
    turned = gather(back_mid.astype(BF16))
    back_attn = turned[0] + turned[1]

    finishing = Scatter(*(after(o, *turned[1][:2]) for o in out1))
    back_attended = back_project(back_attn, w_attn)
    finishing.open(back_attended)
    finishing.near(*out0)
    lse = jnp.concatenate([lse0, lse1], axis=0)
    back_q, back_k, back_v = attend_back(
        query, after(back_attended, *finishing.far), lse, pos_q, keys, values, pos_k
    )
    finishing.take_near(back_q)
    finishing.take()
    if spread > 1:
        shared = lambda t: lax.psum_scatter(
            t, AXES, scatter_dimension=0, tiled=True, axis_index_groups=teams
        )
        back_k, back_v = shared(back_k), shared(back_v)
    joined1, kept, sent = back_input(
        after(back_q, *finishing.sent_far), back_k, back_v, table, w_attn, 1
    )
    entering = Scatter(kept, sent)
    entering.open()
    finishing.pair(joined1)
    joined0, kept, sent = back_input(
        after(back_q, finishing.parts), back_k, back_v, table, w_attn, 0
    )
    entering.near(kept, sent)
    output = mid + finishing.close(joined0)
    block_output = from_micro(output.astype(BF16))
    attn_grads = weight_grads(
        [(normed, [joined0, joined1]), (back_attn, [low0, low1])], width
    )
    entering.take_near(attn_grads)
    entering.take()
    entering.pair()
    feed_sum = collect(after(feed_whole, entering.parts))
    back_normed = entering.close()
    grad_gate, grad_up, grad_down = unpack(scalar(low), feed_sum, (unit,) * 3)
    attn_sum = collect(after(from_groups(after(attn_grads, feed_whole)), back_normed))
    grad_query, grad_key, grad_value, grad_out = unpack(
        scalar(low), attn_sum, (HEAD_DIM,) * 4
    )
    input_grad = from_micro((back_mid + norm_back(back_normed, normed_f, rstd_in)).astype(BF16))
    return (
        block_output,
        input_grad,
        grad_query,
        grad_key,
        grad_value,
        grad_out,
        grad_gate,
        grad_up,
        grad_down,
    )


def solution(mesh):
    rows = P(None, AXES, None)
    tall, wide = P("blk", "head"), P("head", "blk")
    placed = (rows, rows, tall, tall, tall, wide, tall, tall, wide)
    return jax.shard_map(
        functools.partial(local, mesh.shape["blk"], mesh.shape["head"]),
        mesh=mesh,
        in_specs=placed,
        out_specs=placed,
        check_vma=False,
    )
```

```python
import functools

import jax
import jax.numpy as jnp
import numpy as np
from jax import lax
from jax.experimental import pallas as pl
from jax.experimental.pallas import tpu as pltpu
from jax.sharding import PartitionSpec as P

HEADS = 16
HEAD_DIM = 128
FF = 8192
AXES = ("blk", "head")
SCALE = HEAD_DIM**-0.5
EPS = 1e-05
F32 = jnp.float32
BF16 = jnp.bfloat16
VMEM = pl.BlockSpec(memory_space=pltpu.VMEM)
SMEM = pl.BlockSpec(memory_space=pltpu.SMEM)
NN = (((1,), (0,)), ((), ()))
NT = (((1,), (1,)), ((), ()))
TN = (((0,), (0,)), ((), ()))


def dot(a, b, dims=NN):
    return lax.dot_general(a, b, dims, preferred_element_type=F32)


def shape(rows, columns, kind=BF16):
    return jax.ShapeDtypeStruct((rows, columns), kind)


def call(kernel, outs, name, flops=0, moved=0, grid=None, **more):
    settings = dict(
        out_shape=outs,
        compiler_params=pltpu.CompilerParams(vmem_limit_bytes=56 * 2**20),
        name=name,
    )
    if flops:
        settings["cost_estimate"] = pl.CostEstimate(
            flops=int(flops), bytes_accessed=int(moved), transcendentals=0
        )
    settings.update(more)
    if grid is not None:
        settings["grid"] = grid
    return pl.pallas_call(kernel, **settings)


def swap(value, nb, nh, db, dh):
    pairs = [
        (b * nh + h, (b ^ db) * nh + (h ^ dh)) for b in range(nb) for h in range(nh)
    ]
    return lax.ppermute(value, AXES, pairs)


def norm_stats(values):
    center = values - jnp.mean(values, axis=-1, keepdims=True)
    spread = jnp.mean(center * center, axis=-1, keepdims=True)
    rstd = lax.rsqrt(spread + EPS)
    return center * rstd, rstd


def norm_back(grad, normed, rstd):
    return (
        grad
        - jnp.mean(grad, axis=-1, keepdims=True)
        - normed * jnp.mean(grad * normed, axis=-1, keepdims=True)
    ) * rstd


def turn(values, table, back=False):
    half = HEAD_DIM // 2
    other = jnp.concatenate([values[:, half:], values[:, :half]], axis=1)
    other = other * table[:, HEAD_DIM:]
    return values * table[:, :HEAD_DIM] + (-other if back else other)


def after(value, *others):
    return lax.optimization_barrier((value,) + others)[0]


def pack(low, weights, slices, kin):
    wide = [w.shape[1] // slices for w in weights[:-1]]
    wide.append(weights[-1].shape[0] // slices)
    total = sum(wide)

    def kernel(low_ref, *refs):
        sources, outs = refs[: len(weights)], refs[len(weights) :]
        for d in range(slices):
            at = 0
            which = low_ref[0] ^ d
            for i, (source, w) in enumerate(zip(sources, wide)):
                where = pl.ds(pl.multiple_of(which * w, 128), w)
                if i < len(wide) - 1:
                    outs[d][:, at : at + w] = source[:, where]
                else:
                    outs[d][:, at : at + w] = source[where, :].T
                at += w

    return call(
        kernel,
        [shape(kin, total)] * slices,
        "pack",
        in_specs=[SMEM] + [VMEM] * len(weights),
        out_specs=[VMEM] * slices,
    )(low, *weights)


def assemble(low, pieces, kin, slices):
    groups = pieces[0][0].shape[0] // (kin * len(pieces[0][1]))
    total = pieces[0][0].shape[1]

    def kernel(low_ref, *refs):
        out = refs[-1]
        for (_, which), piece in zip(pieces, refs):
            for g in range(groups):
                for i, d in enumerate(which):
                    block = g * slices + (low_ref[0] ^ d)
                    rows = pl.ds(pl.multiple_of(block * kin, kin), kin)
                    at = (g * len(which) + i) * kin
                    out[rows, :] = piece[at : at + kin, :]

    return call(
        kernel,
        shape(groups * slices * kin, total),
        "assemble",
        in_specs=[SMEM] + [VMEM] * len(pieces),
        out_specs=VMEM,
    )(low, *[p for p, _ in pieces])


def unpack(low, pieces, wide):
    kin, slices = pieces[0].shape[0], len(pieces)

    def kernel(low_ref, *refs):
        sources, outs = refs[:slices], refs[slices:]
        for d in range(slices):
            at = 0
            which = low_ref[0] ^ d
            for i, (out, w) in enumerate(zip(outs, wide)):
                where = pl.ds(pl.multiple_of(which * w, 128), w)
                part = sources[d][:, at : at + w].astype(F32)
                if i < len(wide) - 1:
                    out[:, where] = part
                else:
                    out[where, :] = part.T
                at += w

    outs = [shape(kin, slices * w, F32) for w in wide[:-1]]
    outs.append(shape(slices * wide[-1], kin, F32))
    return call(
        kernel,
        outs,
        "unpack",
        in_specs=[SMEM] + [VMEM] * slices,
        out_specs=[VMEM] * len(wide),
    )(low, *pieces)


def join(refs):
    return jnp.concatenate([r[...] for r in refs], axis=0)


def project(pieces, weights, table):
    section = pieces[0].shape[0] * 2
    sections = len(pieces) // 2
    rows = section * sections

    def kernel(*refs):
        parts, (w, t, q, k, v) = refs[: len(pieces)], refs[len(pieces) :]
        for s in range(sections):
            out = dot(join(parts[2 * s : 2 * s + 2]), w[:, : 3 * HEAD_DIM])
            at = pl.ds(s * section, section)
            angles = t[at, :]
            q[at, :] = turn(out[:, :HEAD_DIM], angles).astype(BF16)
            k[at, :] = turn(out[:, HEAD_DIM : 2 * HEAD_DIM], angles).astype(BF16)
            v[at, :] = out[:, 2 * HEAD_DIM :].astype(BF16)

    width = weights.shape[0]
    return call(
        kernel,
        [shape(rows, HEAD_DIM)] * 3,
        "project",
        6 * rows * width * HEAD_DIM,
        2 * rows * width,
        in_specs=[VMEM] * (len(pieces) + 2),
        out_specs=[VMEM] * 3,
    )(*pieces, weights, table)


def row_block(keys, rows):
    return max(64, rows * 2048 // keys)


def split_rows(rows, step, width):
    n = rows // 2 // step
    return (
        n,
        [
            pl.BlockSpec((step, width), lambda i: (jnp.minimum(i, n - 1), 0)),
            pl.BlockSpec((step, width), lambda i: (jnp.maximum(i - n, 0), 0)),
        ],
        [shape(rows // 2, width)] * 2,
    )


def put(n, kept, sent, value):
    @pl.when(pl.program_id(0) < n)
    def _():
        kept[...] = value

    @pl.when(pl.program_id(0) >= n)
    def _():
        sent[...] = value


def attend(q, k, v, weights, pos_q, pos_k, half):
    rows, keys, width = q.shape[0] // 2, k.shape[0], weights.shape[0]
    bq = min(rows // 2, row_block(keys, 256))
    first = half * rows // bq
    n, split, shapes = split_rows(rows, bq, width)

    def kernel(q_ref, k_ref, v_ref, w_ref, pq_ref, pk_ref, o_ref, lse_ref, kept, sent):
        scores = dot(q_ref[...], k_ref[...], NT)
        scores = jnp.where(pk_ref[...] <= pq_ref[...], scores * SCALE, -1e30)
        top = jnp.max(scores, axis=-1, keepdims=True)
        probs = jnp.exp(scores - top)
        total = jnp.sum(probs, axis=-1, keepdims=True)
        low = (dot(probs.astype(BF16), v_ref[...]) / total).astype(BF16)
        o_ref[...] = low
        lse_ref[...] = top + jnp.log(total)
        put(n, kept, sent, dot(low, w_ref[:, 3 * HEAD_DIM :], NT).astype(BF16))

    there = lambda w: pl.BlockSpec((bq, w), lambda i: (i + first, 0))
    here = lambda w: pl.BlockSpec((bq, w), lambda i: (i, 0))
    whole = lambda a: pl.BlockSpec(a.shape, lambda i: (0, 0))
    return call(
        kernel,
        [shape(rows, HEAD_DIM), shape(rows, 1, F32)] + shapes,
        "attend",
        4 * rows * keys * HEAD_DIM + 2 * rows * width * HEAD_DIM,
        2 * rows * width,
        grid=(rows // bq,),
        in_specs=[there(HEAD_DIM), whole(k), whole(v), whole(weights), there(1), whole(pos_k)],
        out_specs=[here(HEAD_DIM), here(1)] + split,
    )(q, k, v, weights, pos_q, pos_k)


def feed(tokens, backs, weights):
    rows, width = sum(p.shape[0] for p in tokens), weights.shape[0]
    unit = weights.shape[1] // 3
    count = len(tokens)
    step = min(512, rows // 2)

    def kernel(*refs):
        xs, gs = refs[:count], refs[count : 2 * count]
        w, paired, hidden, kept, sent, x_all, g_all = refs[2 * count :]
        at = 0
        for x, g in zip(xs, gs):
            x_all[at : at + x.shape[0], :] = x[...]
            g_all[at : at + x.shape[0], :] = g[...]
            at += x.shape[0]

        for first, part in ((0, kept), (rows // 2, sent)):

            @pl.loop(0, rows // 2 // step)
            def _(i):
                at = pl.ds(pl.multiple_of(first + i * step, step), step)
                gate_up = dot(x_all[at, :], w[:, : 2 * unit])
                back = dot(g_all[at, :], w[:, 2 * unit :])
                gate, up = gate_up[:, :unit], gate_up[:, unit:]
                sig = 1.0 / (1.0 + jnp.exp(-gate))
                act = gate * sig
                hidden[at, :] = (act * up).astype(BF16)
                paired[at, :unit] = (back * up * sig * (1.0 + gate * (1.0 - sig))).astype(BF16)
                paired[at, unit:] = (back * act).astype(BF16)
                there = pl.ds(pl.multiple_of(i * step, step), step)
                part[there, :] = dot(paired[at, :], w[:, : 2 * unit], NT).astype(BF16)

    return call(
        kernel,
        [shape(rows, 2 * unit), shape(rows, unit)] + [shape(rows // 2, width)] * 2,
        "feed",
        10 * rows * unit * width,
        2 * rows * width,
        in_specs=[VMEM] * (2 * count + 1),
        out_specs=[VMEM] * 4,
        scratch_shapes=[pltpu.VMEM((rows, width), BF16)] * 2,
    )(*tokens, *backs, weights)


def feed_out(hidden, weights):
    rows, unit = hidden.shape
    width = weights.shape[0]
    step = min(256, rows // 2)
    n, split, shapes = split_rows(rows, step, width)

    def kernel(hidden_ref, w_ref, kept, sent):
        put(n, kept, sent, dot(hidden_ref[...], w_ref[:, 2 * unit :], NT).astype(BF16))

    return call(
        kernel,
        shapes,
        "feed_out",
        2 * rows * unit * width,
        2 * rows * width,
        grid=(rows // step,),
        in_specs=[
            pl.BlockSpec((step, unit), lambda i: (i, 0)),
            pl.BlockSpec(weights.shape, lambda i: (0, 0)),
        ],
        out_specs=split,
    )(hidden, weights)


def weight_grads(pairs, width):
    columns = [sides[0].shape[1] for _, sides in pairs]
    total = sum(columns)
    block = 512
    flat = []
    for pieces, sides in pairs:
        flat += list(pieces) + list(sides)

    def kernel(*refs):
        out = refs[-1]
        at, start = 0, 0
        for (pieces, sides), wide in zip(pairs, columns):
            left = join(refs[at : at + len(pieces)])
            at += len(pieces)
            right = join(refs[at : at + len(sides)])
            at += len(sides)
            out[:, start : start + wide] = dot(left, right, TN).astype(BF16)
            start += wide

    specs = []
    for pieces, sides in pairs:
        specs += [pl.BlockSpec((p.shape[0], block), lambda j: (0, j)) for p in pieces]
        specs += [pl.BlockSpec(s.shape, lambda j: (0, 0)) for s in sides]
    rows = sum(p.shape[0] for p in pairs[0][0])
    return call(
        kernel,
        shape(width, total),
        "weight_grads",
        2 * rows * width * total,
        2 * rows * (width + total),
        grid=(width // block,),
        in_specs=specs,
        out_specs=pl.BlockSpec((block, total), lambda j: (j, 0)),
    )(*flat)


def back_project(pieces, weights):
    rows, width = sum(p.shape[0] for p in pieces), weights.shape[0]

    def kernel(*refs):
        w, out = refs[-2:]
        at = 0
        for s in range(len(pieces) // 2):
            x = join(refs[2 * s : 2 * s + 2])
            out[at : at + x.shape[0], :] = dot(x, w[:, 3 * HEAD_DIM :]).astype(BF16)
            at += x.shape[0]

    return call(
        kernel,
        shape(rows, HEAD_DIM),
        "back_project",
        2 * rows * width * HEAD_DIM,
        2 * rows * width,
        in_specs=[VMEM] * (len(pieces) + 1),
        out_specs=VMEM,
    )(*pieces, weights)


def attend_back(q, dos, lses, pos_q, k, v, pos_k):
    rows, keys = q.shape[0], k.shape[0]
    bq = min(rows // 2, row_block(keys, 512))
    n = rows // 2 // bq

    def kernel(q_ref, *refs):
        do0, do1, lse0, lse1, pq_ref, k_ref, v_ref, pk_ref, dq_ref, dk_ref, dv_ref = refs
        near = pl.program_id(0) < n

        @pl.when(pl.program_id(0) == 0)
        def _():
            dk_ref[...] = jnp.zeros_like(dk_ref)
            dv_ref[...] = jnp.zeros_like(dv_ref)

        q, k, v = q_ref[...], k_ref[...], v_ref[...]
        do = jnp.where(near, do0[...], do1[...])
        lse = jnp.where(near, lse0[...], lse1[...])
        scores = dot(q, k, NT)
        probs = jnp.where(
            pk_ref[...] <= pq_ref[...], jnp.exp(scores * SCALE - lse), 0.0
        )
        dots = dot(do, v, NT)
        delta = jnp.sum(probs * dots, axis=-1, keepdims=True)
        back = (probs * (dots - delta)).astype(BF16)
        dq_ref[...] = dot(back, k) * SCALE
        dk_ref[...] += dot(back, q, TN) * SCALE
        dv_ref[...] += dot(probs.astype(BF16), do, TN)

    row = lambda w: pl.BlockSpec((bq, w), lambda i: (i, 0))
    halves = lambda w: [
        pl.BlockSpec((bq, w), lambda i: (jnp.minimum(i, n - 1), 0)),
        pl.BlockSpec((bq, w), lambda i: (jnp.maximum(i - n, 0), 0)),
    ]
    whole = lambda s: pl.BlockSpec(s, lambda i: (0, 0))
    kv = whole((keys, HEAD_DIM))
    return call(
        kernel,
        [shape(rows, HEAD_DIM, F32), shape(keys, HEAD_DIM, F32), shape(keys, HEAD_DIM, F32)],
        "attend_back",
        10 * rows * keys * HEAD_DIM,
        16 * rows * HEAD_DIM,
        grid=(rows // bq,),
        in_specs=[row(HEAD_DIM)] + halves(HEAD_DIM) + halves(1) + [row(1), kv, kv, whole((1, keys))],
        out_specs=[row(HEAD_DIM), kv, kv],
    )(q, *dos, *lses, pos_q, k, v, pos_k)


def back_input(dq, dk, dv, table, weights, half):
    rows, width = dq.shape[0] // 2, weights.shape[0]
    step = min(256, rows // 2)
    first = half * rows // step
    n, split, shapes = split_rows(rows, step, width)

    def kernel(dq_ref, dk_ref, dv_ref, t_ref, w_ref, joined, kept, sent):
        joined[:, :HEAD_DIM] = turn(dq_ref[...], t_ref[...], True).astype(BF16)
        joined[:, HEAD_DIM : 2 * HEAD_DIM] = turn(dk_ref[...], t_ref[...], True).astype(BF16)
        joined[:, 2 * HEAD_DIM :] = dv_ref[...].astype(BF16)
        put(n, kept, sent, dot(joined[...], w_ref[:, : 3 * HEAD_DIM], NT).astype(BF16))

    there = lambda w: pl.BlockSpec((step, w), lambda i: (i + first, 0))
    here = lambda w: pl.BlockSpec((step, w), lambda i: (i, 0))
    return call(
        kernel,
        [shape(rows, 3 * HEAD_DIM)] + shapes,
        "back_input",
        6 * rows * width * HEAD_DIM,
        2 * rows * width,
        grid=(rows // step,),
        in_specs=[there(HEAD_DIM)] * 3
        + [there(2 * HEAD_DIM), pl.BlockSpec(weights.shape, lambda i: (0, 0))],
        out_specs=[here(3 * HEAD_DIM)] + split,
    )(dq, dk, dv, table, weights)


def local(nb, nh, block_input, cotangent, w_query, w_key, w_value, w_out, w_gate, w_up, w_down):
    tok_rows, width = block_input.shape[1:]
    slices = HEADS // nh
    half = nb // 2
    groups = nb // slices
    spread = groups // 2
    kin = width // nb
    unit = FF // HEADS
    b, h = lax.axis_index("blk"), lax.axis_index("head")
    low, group = b % slices, b // slices
    second = b >= half
    mine = 2 * tok_rows
    move = functools.partial(swap, nb=nb, nh=nh)
    scalar = lambda v: v.astype(jnp.int32).reshape(1)

    opening, core = (2, 0), (0, 1)
    orders = [((1, 0), (0, 2)), ((0, 2), (1, 0))]

    def exchange(values, step):
        return [move(v, db=o[step][0], dh=o[step][1]) for v, o in zip(values, orders)]

    def across(value, way):
        return move(value, db=way[0], dh=way[1])

    def tied(values, beside):
        return [after(v, *beside) for v in values] if beside else values

    class Gather:
        def __init__(self, value):
            self.parts = value
            self.sent = across(value, opening)

        def open(self, *beside):
            arrived = tied([self.sent], beside)[0]
            n = tok_rows
            self.parts = [
                jnp.concatenate([self.parts[:n], arrived[:n]], axis=0),
                jnp.concatenate([self.parts[n:], arrived[n:]], axis=0),
            ]
            self.sent = exchange(self.parts, 0)

        def take(self, *beside):
            arrived = tied(self.sent, beside)
            self.parts = [jnp.concatenate([p, r], axis=0) for p, r in zip(self.parts, arrived)]
            self.sent = exchange(self.parts, 1)
            self.near = self.parts + [across(p, core) for p in self.parts]

        def far(self, *beside):
            pieces = tied(self.sent, beside)
            return pieces + [across(p, core) for p in pieces]

    def gather(value):
        work = Gather(value)
        work.open()
        work.take()
        return work.near, work.far()

    class Scatter:
        def __init__(self, kept, sent):
            self.kept, self.sent = kept, across(sent, core)

        def add(self, *beside):
            arrived = tied([self.sent], beside)[0]
            n = self.kept.shape[0] // 2
            return [
                (self.kept[r].astype(F32) + arrived[r].astype(F32)).astype(BF16)
                for r in (slice(0, n), slice(n, 2 * n))
            ]

        def open(self, *beside):
            self.far = self.add(*beside)
            self.sent_far = exchange(self.far, 1)

        def near(self, kept, sent):
            self.kept, self.sent = kept, across(sent, core)

        def take_near(self, *beside):
            self.parts = self.add(*beside)

        def take(self, *beside):
            arrived = tied(self.sent_far, beside)
            sums = [p.astype(F32) + r.astype(F32) for p, r in zip(self.parts, arrived)]
            n = 2 * tok_rows
            self.parts = [p[:n] for p in sums]
            self.sent = exchange([p[n:].astype(BF16) for p in sums], 0)

        def pair(self, *beside):
            arrived = tied(self.sent, beside)
            sums = [p + r.astype(F32) for p, r in zip(self.parts, arrived)]
            n = tok_rows
            self.parts = jnp.concatenate([p[:n] for p in sums], axis=0)
            self.sent = across(
                jnp.concatenate([p[n:] for p in sums], axis=0).astype(BF16), opening
            )

        def close(self, *beside):
            return self.parts + tied([self.sent], beside)[0].astype(F32)

    flip_b, flip_h, place = [], [], []
    for last in range(2):
        for other in range(2):
            for r, (one, two) in enumerate(orders):
                db, dh = np.array([0, opening[0]]), np.array([0, opening[1]])
                db, dh = np.concatenate([db, db ^ one[0]]), np.concatenate([dh, dh ^ one[1]])
                if last:
                    db, dh = db ^ two[0], dh ^ two[1]
                dh = dh ^ other
                flip_b.append(np.repeat(db, tok_rows) ^ (half if r else 0))
                flip_h.append(np.repeat(dh, tok_rows))
                place.append(np.tile(np.arange(tok_rows), 4))
    flip_b, flip_h, place = (np.concatenate(t).astype(np.int32) for t in (flip_b, flip_h, place))

    def positions(block):
        return ((block ^ flip_b) * nh + (h ^ flip_h)) * tok_rows + place

    pos = positions(b)
    rates = 10000.0 ** (-jnp.arange(HEAD_DIM // 2, dtype=F32) * 2.0 / HEAD_DIM)
    angles = pos.astype(F32)[:, None] * rates[None, :]
    cosine, sine = jnp.cos(angles), jnp.sin(angles)
    table = jnp.concatenate([cosine, cosine, -sine, sine], axis=1)

    def to_micro(pair, *beside):
        keep = jnp.where(second, pair[1], pair[0])
        send = jnp.where(second, pair[0], pair[1])
        arrived = tied([move(send, db=half, dh=0)], beside)[0]
        return jnp.concatenate([keep, arrived], axis=0)

    def from_micro(rows):
        arrived = move(rows[tok_rows:], db=half, dh=0)
        kept = rows[:tok_rows]
        return jnp.stack(
            [jnp.where(second, arrived, kept), jnp.where(second, kept, arrived)]
        )

    alike = [[g * slices + l for g in range(groups)] for l in range(slices)]

    def to_groups(piece):
        return lax.all_gather(piece, "blk", axis=0, tiled=True, axis_index_groups=alike)

    def doubled(piece):
        step = slices
        while step < nb:
            arrived = move(piece, db=step, dh=0)
            upper = (b // step) % 2 == 1
            piece = jnp.where(
                upper,
                jnp.concatenate([arrived, piece], axis=0),
                jnp.concatenate([piece, arrived], axis=0),
            )
            step *= 2
        return piece

    def from_slices(pieces):
        return [move(p, db=d + 1, dh=0) for d, p in enumerate(pieces[1:])]

    def from_groups(grads):
        return lax.psum_scatter(
            grads, "blk", scatter_dimension=0, tiled=True, axis_index_groups=alike
        )

    def collect(whole):
        whole = whole.reshape(slices, kin, -1)
        pick = lambda d: lax.dynamic_index_in_dim(whole, low ^ d, 0, False)
        return [pick(0)] + [move(pick(d), db=d, dh=0) for d in range(1, slices)]

    every = tuple(range(slices))
    attn_own = pack(scalar(low), (w_query, w_key, w_value, w_out), slices, kin)
    feed_own = pack(scalar(low), (w_gate, w_up, w_down), slices, kin)
    tokens = to_micro(block_input, table, *attn_own, *feed_own).astype(F32)
    attn_rest = from_slices(attn_own)
    feed_all = [to_groups(feed_own[0])]
    attn_all = to_groups(
        after(jnp.concatenate([attn_own[0]] + attn_rest, axis=0), *feed_all)
    )
    w_attn = assemble(scalar(low), [(attn_all, every)], kin, slices)
    normed_f, rstd_in = norm_stats(tokens)
    first = Gather(normed_f.astype(BF16))
    back_rows = to_micro(cotangent)
    first.open(*attn_rest, back_rows)
    feed_rest = from_slices(feed_own)
    first.take()
    normed = first.near + first.far(*feed_rest)
    for piece in (feed_rest[1], feed_rest[0]):
        feed_all.append(to_groups(piece))
    feed_all.append(doubled(feed_rest[2]))
    cots = Gather(after(back_rows, *normed[:2]))
    query, key, value = project(normed, w_attn, table)
    if spread > 1:
        teams = [
            [(((m * spread + s) * slices + l) * nh + k) for s in range(spread)]
            for m in range(2)
            for l in range(slices)
            for k in range(nh)
        ]
        everyone = lambda t: lax.all_gather(t, AXES, axis=0, tiled=True, axis_index_groups=teams)
        keys, values = everyone(key), everyone(value)
        first = b - (group % spread) * slices
        pos_k = jnp.concatenate([positions(first + s * slices) for s in range(spread)])
    else:
        keys, values, pos_k = key, value, pos

    pos_q, pos_k = pos[:, None], pos_k[None, :]
    low1, lse1, kept, sent = attend(query, keys, values, w_attn, pos_q, pos_k, 1)
    mixing = Scatter(kept, sent)
    mixing.open()
    low0, lse0, kept, sent = attend(
        after(query, *mixing.far, cots.sent), keys, values, w_attn, pos_q, pos_k, 0
    )
    cots.open()
    mixing.near(kept, sent)
    mixing.take_near()
    mixing.take(feed_all[1])
    cots.take(*mixing.parts)
    mixing.pair()
    mid = tokens + mixing.close(feed_all[2], feed_all[3])
    mid_f, rstd_mid = norm_stats(mid)

    mids = Gather(mid_f.astype(BF16))
    mids.open(*cots.sent)
    backs_far = cots.far(*mids.parts)
    backs_near = cots.near
    mids.take(*backs_far)
    w_feed = assemble(
        scalar(low),
        [(a, d) for a, d in zip(feed_all, ((0,), (2,), (1,), (3,)))],
        kin,
        slices,
    )
    paired0, hidden0, kept0, sent0 = feed(mids.near, backs_near, w_feed)
    mids_far = mids.far(hidden0)
    paired1, hidden1, kept, sent = feed(mids_far, backs_far, w_feed)
    giving = Scatter(kept, sent)
    giving.open()
    giving.near(kept0, sent0)
    feed_grads = weight_grads(
        [
            (mids.near + mids_far, [paired0, after(paired1, *giving.far)]),
            (backs_near + backs_far, [hidden0, hidden1]),
        ],
        width,
    )
    giving.take_near()
    giving.take(feed_grads)
    feed_whole = from_groups(feed_grads)
    out1 = feed_out(after(hidden1, *giving.parts), w_feed)
    giving.pair(*out1)
    out0 = feed_out(after(hidden0, giving.parts), w_feed)
    back_mid_normed = giving.close(*out0)

    back_mid = back_rows.astype(F32) + norm_back(back_mid_normed, mid_f, rstd_mid)
    turned = gather(back_mid.astype(BF16))
    back_attn = turned[0] + turned[1]

    finishing = Scatter(*(after(o, *turned[1][:2]) for o in out1))
    back_near = back_project(turned[0], w_attn)
    back_far = back_project([after(turned[1][0], back_near)] + turned[1][1:], w_attn)
    finishing.open(back_far)
    finishing.near(*out0)
    back_q, back_k, back_v = attend_back(
        query,
        (back_near, after(back_far, *finishing.far)),
        (lse0, lse1),
        pos_q,
        keys,
        values,
        pos_k,
    )
    finishing.take_near(back_q)
    finishing.take()
    if spread > 1:
        shared = lambda t: lax.psum_scatter(
            t, AXES, scatter_dimension=0, tiled=True, axis_index_groups=teams
        )
        back_k, back_v = shared(back_k), shared(back_v)
    joined1, kept, sent = back_input(
        after(back_q, *finishing.sent_far), back_k, back_v, table, w_attn, 1
    )
    entering = Scatter(kept, sent)
    entering.open()
    finishing.pair(joined1)
    joined0, kept, sent = back_input(
        after(back_q, finishing.parts), back_k, back_v, table, w_attn, 0
    )
    entering.near(kept, sent)
    output = mid + finishing.close(joined0)
    block_output = from_micro(output.astype(BF16))
    attn_grads = weight_grads(
        [(normed, [joined0, joined1]), (back_attn, [low0, low1])], width
    )
    entering.take_near(attn_grads)
    entering.take()
    entering.pair()
    feed_sum = collect(after(feed_whole, entering.parts))
    back_normed = entering.close()
    grad_gate, grad_up, grad_down = unpack(scalar(low), feed_sum, (unit,) * 3)
    attn_sum = collect(after(from_groups(after(attn_grads, feed_whole)), back_normed))
    grad_query, grad_key, grad_value, grad_out = unpack(
        scalar(low), attn_sum, (HEAD_DIM,) * 4
    )
    input_grad = from_micro((back_mid + norm_back(back_normed, normed_f, rstd_in)).astype(BF16))
    return (
        block_output,
        input_grad,
        grad_query,
        grad_key,
        grad_value,
        grad_out,
        grad_gate,
        grad_up,
        grad_down,
    )


def solution(mesh):
    rows = P(None, AXES, None)
    tall, wide = P("blk", "head"), P("head", "blk")
    placed = (rows, rows, tall, tall, tall, wide, tall, tall, wide)
    return jax.shard_map(
        functools.partial(local, mesh.shape["blk"], mesh.shape["head"]),
        mesh=mesh,
        in_specs=placed,
        out_specs=placed,
        check_vma=False,
    )
```
